32 devices in a mesh: rec: 8 (over z, y), src: 4 (over x, core).
Axes of the slice: x: 2, y: 2, z: 4, core: 2. Of those that a mesh axis runs over, the one named last changes fastest.
Arguments:
- kernel: float32 [2, 2, 5120, 5120], P(None, None, 'rec', 'src'), may hold values from -0.0625 to 0.0625
- traces: float32 [4, 2560, 2, 2, 256], P('src', 'rec')
- acq_lists: int32 [4, 2560], P('src', 'rec'), may hold values from 0 to 1279, as said below
- counts: int32 [4, 8], P('src', 'rec'), may hold values from 1 to 320, as said below
Outputs:
- solution: float32 [5120, 2, 2, 256], P(('src', 'rec'))
- next_left: float32 [5120, 2, 2, 256], P(('rec', 'src'))
The draws below stay inside these ranges and needn't reach their ends.
Inputs may be any that keep to these rules, and one draw needn't show every extreme that they name: `acq_lists`: an id a * 160 + k names row k of area a. Within each list the first counts[s, r] slots of the blocks name every id exactly once; other slots hold ids to be ignored. No block names more than 40 ids of one area, and every block that names an area names exactly 40 of its ids. `counts`: used slots of a block; in every list some block uses all 320.
All inputs are finite; a program needn't handle non-finite values.
Results may differ from the reference program's by a relative error of at most 0.00026.
Values sent between devices are 32-bit elements; how exact they have to be, the bound alone decides.
No kernel may reach another device: no remote copies, remote signals or barrier semaphores. Data moves between devices by JAX's collectives and lax.ppermute only.
A program may use at most 128 MiB of HBM per device.

```python
import math
import jax
import jax.numpy as jnp
from jax import lax

NR = 5120
FREQS = 2
SOURCES = 256
ITERS = 2
AREAS = 8
LISTS = 4
ROWS = 160
PEER = 40
GROUPS = 4
HEAVY = 2
CAP = 320


def one_list(list_key):
    keys = jax.random.split(list_key, 6)
    heavy_count = AREAS // 4
    light_count = AREAS - heavy_count
    total_rows = AREAS * ROWS
    shuffled = jax.random.permutation(keys[0], AREAS)
    heavy = shuffled[:heavy_count]
    light = shuffled[heavy_count:]
    heavy_shift = jax.random.permutation(keys[1], heavy_count)[:HEAVY]
    light_shift = jax.random.permutation(keys[3], light_count)[:GROUPS - HEAVY]
    area_index = jnp.arange(AREAS, dtype=jnp.int32)
    senders = jnp.concatenate([heavy[(area_index[:, None] + heavy_shift[None, :]) % heavy_count], light[(area_index[:, None] + light_shift[None, :]) % light_count]], axis=1)
    row_keys = jax.random.split(keys[4], AREAS)
    group_of_row = jax.vmap(lambda row_key: jax.random.permutation(row_key, ROWS))(row_keys) // PEER
    sender_of = jnp.take_along_axis(senders, group_of_row, axis=1).reshape(-1).astype(jnp.int32)
    identity = jnp.arange(total_rows, dtype=jnp.int32)
    tiebreak = jax.random.permutation(keys[5], total_rows).astype(jnp.int32)
    arranged = jnp.argsort(sender_of * total_rows + tiebreak, stable=True)
    sorted_sender = sender_of[arranged]
    sorted_id = identity[arranged]
    block_counts = jnp.sum((sender_of[None, :] == area_index[:, None]).astype(jnp.int32), axis=1)
    starts = jnp.cumsum(block_counts) - block_counts
    slot_place = identity - starts[sorted_sender]
    filler = jax.random.randint(jax.random.fold_in(list_key, 9), (AREAS, CAP), 0, total_rows)
    table = filler.at[sorted_sender, slot_place].set(sorted_id)
    return (table.reshape(-1).astype(jnp.int32), block_counts.astype(jnp.int32))


def acquisition(base_key):
    list_keys = jax.random.split(base_key, LISTS)
    return jax.vmap(one_list)(list_keys)


def draw_acq_lists(key, part):
    return acquisition(jax.random.fold_in(key, 11))[0]


def draw_counts(key, part):
    return acquisition(jax.random.fold_in(key, 11))[1]


def draw_traces(key, part):
    list_ids = acquisition(jax.random.fold_in(key, 11))[0]
    keys = jax.random.split(jax.random.fold_in(key, 23), 3)
    row_scale = jnp.exp(jax.random.uniform(keys[0], (LISTS, AREAS * ROWS), jnp.float32, 0.0, math.log(10.0)))
    slot_scale = jnp.take_along_axis(row_scale, list_ids, axis=1)
    rising = 1.0 + 2.0 * (list_ids // ROWS).astype(jnp.float32) / (AREAS - 1)
    source_scale = jnp.exp(jax.random.uniform(keys[1], (SOURCES,), jnp.float32, 0.0, math.log(10.0)))
    shape = (LISTS, AREAS * CAP, 2, FREQS, SOURCES)
    base = jax.random.normal(keys[2], shape, jnp.float32)
    values = 0.1 * base * (slot_scale * rising)[:, :, None, None, None] * source_scale[None, None, None, None, :]
    return values.astype(jnp.float32)


def steps_of(own_key, dims, cuts, low, high):
    gain, own = 1.0, jax.random.fold_in(own_key, 6)
    for dim, shards_of in cuts:
        heights = jnp.exp(jax.random.uniform(jax.random.fold_in(own, dim), (shards_of,), jnp.float32, low / len(cuts), high / len(cuts)))
        gain = gain * jnp.repeat(heights, dims[dim] // shards_of).reshape([-1 if axis == dim else 1 for axis in range(len(dims))])
    return gain


def normal_values(rng, extent, spread, reach, cuts=(), kind=jnp.bfloat16):
    factor_of = steps_of(rng, extent, cuts, -0.22, 0.18) if cuts else 1.0
    entries = jax.random.normal(rng, extent, jnp.float32) * spread * factor_of
    return jnp.minimum(jnp.maximum(entries, -reach), reach).astype(kind)


def setup_inputs(seed: int = 0) -> dict:
    streams_of = jax.random.split(jax.random.key(seed), 5)
    return {
        "kernel": normal_values(streams_of[0], (2, FREQS, NR, NR), (2 * NR) ** -0.5, 0.0625, ((2, 8), (3, 4)), jnp.float32),
        "traces": draw_traces(jax.random.fold_in(streams_of[4], 71), 0),
        "acq_lists": draw_acq_lists(jax.random.fold_in(streams_of[4], 71), 0),
        "counts": draw_counts(jax.random.fold_in(streams_of[4], 71), 0),
    }


def kernel_apply(kernel, vector):
    highest = lax.Precision.HIGHEST
    real_part = jnp.einsum('fmc,cfn->mfn', kernel[0], vector[:, 0], precision=highest) - jnp.einsum('fmc,cfn->mfn', kernel[1], vector[:, 1], precision=highest)
    imag_part = jnp.einsum('fmc,cfn->mfn', kernel[0], vector[:, 1], precision=highest) + jnp.einsum('fmc,cfn->mfn', kernel[1], vector[:, 0], precision=highest)
    return jnp.stack([real_part, imag_part], axis=1)

def kernel_adjoint(kernel, vector):
    highest = lax.Precision.HIGHEST
    real_part = jnp.einsum('fmc,mfn->cfn', kernel[0], vector[:, 0], precision=highest) + jnp.einsum('fmc,mfn->cfn', kernel[1], vector[:, 1], precision=highest)
    imag_part = jnp.einsum('fmc,mfn->cfn', kernel[0], vector[:, 1], precision=highest) - jnp.einsum('fmc,mfn->cfn', kernel[1], vector[:, 0], precision=highest)
    return jnp.stack([real_part, imag_part], axis=1)

def rms_norm(vector):
    return jnp.sqrt(lax.optimization_barrier(jnp.sum(vector * vector, axis=(0, 1, 3))) / (2.0 * NR * SOURCES))

def widen(values):
    return values[None, None, :, None]

def reference(kernel, traces, acq_lists, counts):
    slot_index = jnp.arange(AREAS * CAP, dtype=jnp.int32)
    block_index = slot_index // CAP
    filled = (slot_index % CAP)[None, :] < counts[:, block_index]
    list_index = jnp.arange(LISTS, dtype=jnp.int32)[:, None]
    target = (acq_lists // ROWS * LISTS + list_index) * ROWS + acq_lists % ROWS
    target = jnp.where(filled, target, NR).astype(jnp.int32)
    observed = jnp.zeros((NR + 1, 2, FREQS, SOURCES), jnp.float32)
    observed = observed.at[target.reshape(-1)].add(traces.reshape(-1, 2, FREQS, SOURCES))[:NR]
    beta_norm = rms_norm(observed)
    left_unit = observed / widen(beta_norm)
    right_vec = kernel_adjoint(kernel, left_unit)
    alpha_norm = rms_norm(right_vec)
    right_unit = right_vec / widen(alpha_norm)
    search = right_unit
    solution = jnp.zeros((NR, 2, FREQS, SOURCES), jnp.float32)
    phibar = beta_norm
    rhobar = alpha_norm
    next_left = observed
    for iteration in range(ITERS):
        next_left = kernel_apply(kernel, right_unit) - widen(alpha_norm) * left_unit
        beta_norm = rms_norm(next_left)
        left_unit = next_left / widen(beta_norm)
        rho_value = jnp.sqrt(rhobar * rhobar + beta_norm * beta_norm)
        cosine = rhobar / rho_value
        sine_value = beta_norm / rho_value
        phi_value = cosine * phibar
        phibar = sine_value * phibar
        solution = solution + widen(phi_value / rho_value) * search
        if iteration + 1 < ITERS:
            right_vec = kernel_adjoint(kernel, left_unit) - widen(beta_norm) * right_unit
            alpha_norm = rms_norm(right_vec)
            right_unit = right_vec / widen(alpha_norm)
            theta_value = sine_value * alpha_norm
            rhobar = -cosine * alpha_norm
            search = right_unit - widen(theta_value / rho_value) * search
    return (solution, next_left)
```

```python
import functools
import jax
import jax.numpy as jnp
from jax import lax
from jax.experimental import pallas as pl
from jax.experimental.pallas import tpu as pltpu
from jax.sharding import Mesh, PartitionSpec as P

FREQS = 2
SOURCES = 256
ITERS = 2
HEAD = 8
REC = ("z", "y")
SRC = ("x", "c")
VMEM_BYTES = 50 * 2**20


def split(values):
    high = values.astype(jnp.bfloat16)
    return high, (values - high.astype(jnp.float32)).astype(jnp.bfloat16)


def dot_three(left, right, dims):
    def dot(a, b):
        return lax.dot_general(a, b, (dims, ((), ())), preferred_element_type=jnp.float32)

    return dot(left[0], right[0]) + (dot(left[0], right[1]) + dot(left[1], right[0]))


def dot_exact(chosen, values):
    total = None
    for _ in range(3):
        part = values.astype(jnp.bfloat16)
        values = values - part.astype(jnp.float32)
        term = lax.dot_general(
            chosen, part, (((0,), (0,)), ((), ())), preferred_element_type=jnp.float32
        )
        total = term if total is None else total + term
    return total


def xor_index(axis, k):
    index = lax.axis_index(axis)
    if k == 0:
        return index
    if k == 1:
        return index + 1 - 2 * lax.rem(index, 2)
    if k == 3:
        return 3 - index
    return lax.rem(index + 2, 4)


def product_kernel(adjoint, places, outs, k_ref, *refs):
    piece_refs = refs[: len(places)]
    out_refs = refs[len(places) : len(places) + len(outs)]
    head, high, low, total = refs[len(places) + len(outs) :]
    step = pl.program_id(0)

    @pl.when(step == 0)
    def _():
        sums = None
        for place, piece in zip(places, piece_refs):
            rows = piece.shape[0] - HEAD
            at = 0 if place is None else pl.multiple_of(place() * rows, rows)
            top, bottom = split(piece[HEAD:, :])
            high[pl.ds(at, rows), :] = top
            low[pl.ds(at, rows), :] = bottom
            sums = piece[:HEAD, :] if sums is None else sums + piece[:HEAD, :]
        head[...] = sums

    dims = ((0,), (0,)) if adjoint else ((1,), (0,))
    vector = (high[...], low[...])
    with_real = dot_three(split(k_ref[0, 0]), vector, dims)
    with_imag = dot_three(split(k_ref[1, 0]), vector, dims)
    rows, half = with_real.shape[0], with_real.shape[1] // 2
    at = pl.multiple_of(step * rows, rows)
    if adjoint:
        total[pl.ds(at, rows), :half] = with_real[:, :half] + with_imag[:, half:]
        total[pl.ds(at, rows), half:] = with_real[:, half:] - with_imag[:, :half]
    else:
        total[pl.ds(at, rows), :half] = with_real[:, :half] - with_imag[:, half:]
        total[pl.ds(at, rows), half:] = with_real[:, half:] + with_imag[:, :half]

    @pl.when(step == pl.num_programs(0) - 1)
    def _():
        for out, out_ref in zip(outs, out_refs):
            for slot, place in enumerate(out):
                target = out_ref.at[slot] if len(out) > 1 else out_ref
                rows = target.shape[0] - HEAD
                at = 0 if place is None else pl.multiple_of(place() * rows, rows)
                target[:HEAD, :] = head[...]
                target[HEAD:, :] = total[pl.ds(at, rows), :]


def product(kernel, slab, adjoint, pieces, places, outs, out_rows):
    rows, columns = kernel.shape[2:]
    width = pieces[0].shape[1]
    if adjoint:
        tile = columns // 2 if columns % 256 == 0 and columns > 640 else columns
        steps, shape, given, made = columns // tile, (2, 1, rows, tile), rows, columns
        k_spec = pl.BlockSpec(shape, lambda i: (0, slab, 0, i))
    else:
        tile = rows // 4
        steps, shape, given, made = rows // tile, (2, 1, tile, columns), columns, rows
        k_spec = pl.BlockSpec(shape, lambda i: (0, slab, i, 0))
    shapes = [
        ((len(out),) if len(out) > 1 else ()) + (out_rows + HEAD, width) for out in outs
    ]
    return pl.pallas_call(
        functools.partial(product_kernel, adjoint, places, outs),
        grid=(steps,),
        in_specs=[k_spec] + [pl.BlockSpec(p.shape, lambda i: (0, 0)) for p in pieces],
        out_specs=[pl.BlockSpec(s, lambda i, n=len(s): (0,) * n) for s in shapes],
        out_shape=[jax.ShapeDtypeStruct(s, jnp.float32) for s in shapes],
        scratch_shapes=[
            pltpu.VMEM((HEAD, width), jnp.float32),
            pltpu.VMEM((given, width), jnp.bfloat16),
            pltpu.VMEM((given, width), jnp.bfloat16),
            pltpu.VMEM((made, width), jnp.float32),
        ],
        compiler_params=pltpu.CompilerParams(vmem_limit_bytes=VMEM_BYTES),
        cost_estimate=pl.CostEstimate(
            flops=2 * 3 * 2 * rows * columns * width,
            bytes_accessed=8 * rows * columns + 4 * width * (rows + columns),
            transcendentals=0,
        ),
    )(kernel, *pieces)


def finish_kernel(count, parts, *refs):
    part_refs, refs = refs[:parts], refs[parts:]
    piece_ref, norm_ref = refs[-2:]
    total = part_refs[0][...]
    for part in part_refs[1:]:
        total = total + part[...]
    norm = jnp.sqrt(total[:1, :1] / count)
    data = total[HEAD:, :] / norm
    if len(refs) > 2:
        other, last_norm = refs[:2]
        data = data - norm * (other[HEAD:, :] / last_norm[:1, :1])
    piece_ref[HEAD:, :] = data
    piece_ref[:HEAD, :] = jnp.broadcast_to(jnp.sum(data * data), (HEAD, data.shape[1]))
    norm_ref[...] = jnp.broadcast_to(norm, norm_ref.shape)


def finish(count, parts, *other):
    shape = parts[0].shape
    return pl.pallas_call(
        functools.partial(finish_kernel, count, len(parts)),
        out_shape=[
            jax.ShapeDtypeStruct(shape, jnp.float32),
            jax.ShapeDtypeStruct((8, 128), jnp.float32),
        ],
        compiler_params=pltpu.CompilerParams(vmem_limit_bytes=VMEM_BYTES),
        cost_estimate=pl.CostEstimate(
            flops=shape[0] * shape[1] * 8,
            bytes_accessed=4 * shape[0] * shape[1] * (len(parts) + 2),
            transcendentals=0,
        ),
    )(*parts, *other)


def pack_kernel(place_ref, mark_ref, traces_ref, first_ref, second_ref):
    slots = first_ref.shape[0]
    spots = lax.broadcasted_iota(jnp.int32, (place_ref.shape[0], slots), 1)
    chosen = (place_ref[...] == spots).astype(jnp.bfloat16)
    width = second_ref.shape[1]
    half = width // 2
    packed = dot_exact(chosen, traces_ref[...])
    marks = jnp.broadcast_to(mark_ref[...], (mark_ref.shape[0], 128))
    first_ref[:, :half] = packed[:, :half]
    first_ref[:, half:width] = packed[:, width : width + half]
    first_ref[:, width:] = dot_exact(chosen, marks)
    second_ref[:, :half] = packed[:, half:width]
    second_ref[:, half:] = packed[:, width + half :]


def unpack_kernel(data_ref, mark_ref, piece_ref):
    rows = piece_ref.shape[0] - HEAD
    width = piece_ref.shape[1]
    slots = data_ref.shape[0]
    spots = lax.broadcasted_iota(jnp.int32, (slots, rows), 1) + 1
    chosen = (mark_ref[:, :1].astype(jnp.int32) == spots).astype(jnp.bfloat16)
    data = dot_exact(chosen, data_ref[:, :width])
    piece_ref[HEAD:, :] = data
    piece_ref[:HEAD, :] = jnp.broadcast_to(jnp.sum(data * data), (HEAD, width))


def dispatch(traces, acq_lists, counts, row_count):
    areas = lax.axis_size("z") * lax.axis_size("y")
    slot_count = traces.shape[1]
    width = traces.shape[2] * traces.shape[4]
    peer = -(-slot_count // areas)
    ids = acq_lists[0]
    slot_iota = jnp.arange(slot_count, dtype=jnp.int32)
    area = jnp.where(slot_iota < counts[0, 0], ids // row_count, -1)
    before = (area[:, None] == area[None, :]) & (slot_iota[None, :] < slot_iota[:, None])
    rank = jnp.sum(before.astype(jnp.int32), axis=1)
    place = jnp.where(area >= 0, area * peer + rank, -1)
    mark = (ids % row_count + 1).astype(jnp.float32)
    params = pltpu.CompilerParams(vmem_limit_bytes=VMEM_BYTES)
    slots = areas * peer
    first, second = pl.pallas_call(
        pack_kernel,
        out_shape=[
            jax.ShapeDtypeStruct((slots, width + 128), jnp.float32),
            jax.ShapeDtypeStruct((slots, width), jnp.float32),
        ],
        compiler_params=params,
    )(place[:, None], mark[:, None], traces.reshape(slot_count, -1))

    def exchange(packed):
        packed = packed.reshape(areas, peer, -1)
        packed = lax.all_to_all(packed, REC, 0, 0, tiled=True)
        return packed.reshape(slots, -1)

    unpack = pl.pallas_call(
        unpack_kernel,
        out_shape=jax.ShapeDtypeStruct((row_count + HEAD, width), jnp.float32),
        compiler_params=params,
    )
    first = exchange(first)
    marks = first[:, width:]
    second = exchange(second)
    return [unpack(first, marks), unpack(second, marks)]


def swap(values, axis, k=1):
    size = lax.axis_size(axis)
    return lax.ppermute(values, axis, [(i, i ^ k) for i in range(size)])


def rec_place(kz, ky):
    return lambda: xor_index("z", kz) * 2 + xor_index("y", ky)


def src_place(kx, kc):
    return lambda: xor_index("x", kx) * 2 + xor_index("c", kc)


class Neighbours:
    def gather_src(self, piece, slab):
        x = swap(piece, "x")
        c = swap(piece, "c")
        xc = swap(x, "c")
        return [piece, x, c, xc], [src_place(*k) for k in ((0, 0), (1, 0), (0, 1), (1, 1))]

    def gather_rec(self, piece, slab):
        one, three, side = swap(piece, "z", 1), swap(piece, "z", 3), swap(piece, "y")
        two = swap(three, "z", 1)
        side_three = swap(side, "z", 3)
        side_one = swap(one, "y")
        side_two = swap(two, "y") if slab == 0 else swap(side_three, "z", 1)
        order = ((0, 0), (1, 0), (3, 0), (2, 0), (0, 1), (1, 1), (3, 1), (2, 1))
        return [piece, one, three, two, side, side_one, side_three, side_two], [
            rec_place(*k) for k in order
        ]

    rec_outs = [[rec_place(*k)] for k in ((2, 1), (3, 1), (1, 1), (2, 0))] + [
        [rec_place(*k)] for k in ((0, 0), (1, 0), (3, 0), (0, 1))
    ]
    src_outs = [[src_place(0, 1), src_place(1, 1)], [src_place(1, 0)], [src_place(0, 0)]]

    def scatter_rec(self, blocks, slab):
        side_two, side_three, side_one, two, own, one, three, side = blocks
        if slab == 0:
            two = two + swap(side_two, "y")
        else:
            side_three = side_three + swap(side_two, "z", 1)
        one = one + swap(side_one, "y")
        side = side + swap(side_three, "z", 3)
        three = three + swap(two, "z", 1)
        return [own, swap(one, "z", 1), swap(three, "z", 3), swap(side, "y")]

    def scatter_src(self, blocks, slab):
        sent, across, own = blocks
        back = swap(sent, "c")
        return [own, back[0], swap(across + back[1], "x")]


class Whole:
    rec_outs = [[None]]
    src_outs = [[None]]

    def gather(self, piece, axes):
        pieces = lax.all_gather(piece, axes, axis=0, tiled=False)
        data = pieces[:, HEAD:].reshape(-1, piece.shape[1])
        return [jnp.concatenate([jnp.sum(pieces[:, :HEAD], axis=0), data], axis=0)], [None]

    def scatter(self, blocks, axes):
        count = lax.axis_size(axes[0]) * lax.axis_size(axes[1])
        width = blocks[0].shape[1]
        head = jnp.broadcast_to(blocks[0][:HEAD], (count, HEAD, width))
        data = blocks[0][HEAD:].reshape(count, -1, width)
        both = jnp.concatenate([head, data], axis=1)
        return [lax.psum_scatter(both, axes, scatter_dimension=0, tiled=False)]

    def gather_src(self, piece, slab):
        return self.gather(piece, SRC)

    def gather_rec(self, piece, slab):
        return self.gather(piece, REC)

    def scatter_rec(self, blocks, slab):
        return self.scatter(blocks, REC)

    def scatter_src(self, blocks, slab):
        return self.scatter(blocks, SRC)


def global_sum(values):
    for axis in ("c", "x", "y", "z"):
        k = 1
        while k < lax.axis_size(axis):
            values = values + swap(values, axis, 2 * k - 1)
            k *= 2
    return values


def on_device(kernel, traces, acq_lists, counts):
    sizes = tuple(lax.axis_size(axis) for axis in ("z", "y", "x", "c"))
    row_count = kernel.shape[2] // (sizes[2] * sizes[3])
    column_count = kernel.shape[3] // (sizes[0] * sizes[1])
    aligned = row_count % 16 == 0 and column_count % 16 == 0
    moves = Neighbours() if sizes == (4, 2, 2, 2) and aligned else Whole()
    count = 2.0 * kernel.shape[2] * sizes[0] * sizes[1] * SOURCES

    def adjoint(piece, slab):
        pieces, places = moves.gather_src(piece, slab)
        rows = column_count if len(moves.rec_outs) > 1 else kernel.shape[3]
        blocks = product(kernel, slab, True, pieces, places, moves.rec_outs, rows)
        return moves.scatter_rec(blocks, slab)

    def forward(piece, slab):
        pieces, places = moves.gather_rec(piece, slab)
        rows = row_count if len(moves.src_outs) > 1 else kernel.shape[2]
        blocks = product(kernel, slab, False, pieces, places, moves.src_outs, rows)
        return moves.scatter_src(blocks, slab)

    observed = dispatch(traces, acq_lists, counts, row_count)
    solutions, lefts = [], []
    for slab in range(FREQS):
        left = observed[slab]
        right, beta = finish(count, adjoint(left, slab))
        phibar = beta[0, 0]
        search = None
        for iteration in range(ITERS):
            left, alpha = finish(count, forward(right, slab), left, beta)
            unit = right[HEAD:] / alpha[0, 0]
            if iteration == 0:
                rhobar = alpha[0, 0]
                search = unit
            else:
                rhobar = -cosine * alpha[0, 0]
                search = unit - (sine * alpha[0, 0] / rho) * search
            if iteration + 1 < ITERS:
                right, beta = finish(count, adjoint(left, slab), right, alpha)
                beta_norm = beta[0, 0]
            else:
                beta_norm = jnp.sqrt(global_sum(left[:HEAD, :128])[0, 0] / count)
            rho = jnp.sqrt(rhobar * rhobar + beta_norm * beta_norm)
            cosine = rhobar / rho
            sine = beta_norm / rho
            phi = cosine * phibar
            phibar = sine * phibar
            step = (phi / rho) * search
            solution = step if iteration == 0 else solution + step
        solutions.append(solution)
        lefts.append(left[HEAD:])

    def joined(parts):
        return jnp.stack([p.reshape(p.shape[0], 2, SOURCES) for p in parts], axis=2)

    return joined(solutions), joined(lefts)


def solution(mesh):
    rec, src = mesh.shape["rec"], mesh.shape["src"]
    depth = src // 2
    fine = Mesh(
        mesh.devices.reshape(rec // depth, depth, depth, 2), REC + SRC
    )
    placed = (
        P(None, None, REC, SRC),
        P(SRC, REC, None, None, None),
        P(SRC, REC),
        P(SRC, REC),
    )
    return jax.shard_map(
        on_device,
        mesh=fine,
        in_specs=placed,
        out_specs=(P(SRC + REC, None, None, None), P(REC + SRC, None, None, None)),
        check_vma=False,
    )
```

```python
import functools
import jax
import jax.numpy as jnp
from jax import lax
from jax.experimental import pallas as pl
from jax.experimental.pallas import tpu as pltpu
from jax.sharding import Mesh, PartitionSpec as P

FREQS = 2
SOURCES = 256
ITERS = 2
HEAD = 8
REC = ("z", "y")
SRC = ("x", "c")
VMEM_BYTES = 50 * 2**20


def split(values):
    high = values.astype(jnp.bfloat16)
    return high, (values - high.astype(jnp.float32)).astype(jnp.bfloat16)


def dot_three(left, right, dims):
    def dot(a, b):
        return lax.dot_general(a, b, (dims, ((), ())), preferred_element_type=jnp.float32)

    return dot(left[0], right[0]) + (dot(left[0], right[1]) + dot(left[1], right[0]))


def dot_exact(chosen, values):
    total = None
    for _ in range(3):
        part = values.astype(jnp.bfloat16)
        values = values - part.astype(jnp.float32)
        term = lax.dot_general(
            chosen, part, (((0,), (0,)), ((), ())), preferred_element_type=jnp.float32
        )
        total = term if total is None else total + term
    return total


def other(axis):
    index = lax.axis_index(axis)
    return index + 1 - 2 * lax.rem(index, 2)


def product_kernel(adjoint, places, outs, k_ref, *refs):
    piece_refs = refs[: len(places)]
    out_refs = refs[len(places) : len(places) + len(outs)]
    head, high, low, total = refs[len(places) + len(outs) :]
    step = pl.program_id(0)

    @pl.when(step == 0)
    def _():
        sums = None
        for place, piece in zip(places, piece_refs):
            rows = piece.shape[0] - HEAD
            at = 0 if place is None else pl.multiple_of(place() * rows, rows)
            top, bottom = split(piece[HEAD:, :])
            high[pl.ds(at, rows), :] = top
            low[pl.ds(at, rows), :] = bottom
            sums = piece[:HEAD, :] if sums is None else sums + piece[:HEAD, :]
        head[...] = sums

    dims = ((0,), (0,)) if adjoint else ((1,), (0,))
    vector = (high[...], low[...])
    with_real = dot_three(split(k_ref[0, 0]), vector, dims)
    with_imag = dot_three(split(k_ref[1, 0]), vector, dims)
    rows, half = with_real.shape[0], with_real.shape[1] // 2
    at = pl.multiple_of(step * rows, rows)
    if adjoint:
        total[pl.ds(at, rows), :half] = with_real[:, :half] + with_imag[:, half:]
        total[pl.ds(at, rows), half:] = with_real[:, half:] - with_imag[:, :half]
    else:
        total[pl.ds(at, rows), :half] = with_real[:, :half] - with_imag[:, half:]
        total[pl.ds(at, rows), half:] = with_real[:, half:] + with_imag[:, :half]

    @pl.when(step == pl.num_programs(0) - 1)
    def _():
        for out, out_ref in zip(outs, out_refs):
            for slot, place in enumerate(out):
                target = out_ref.at[slot] if len(out) > 1 else out_ref
                rows = target.shape[0] - HEAD
                at = 0 if place is None else pl.multiple_of(place() * rows, rows)
                target[:HEAD, :] = head[...]
                target[HEAD:, :] = total[pl.ds(at, rows), :]


def product(kernel, slab, adjoint, pieces, places, outs, out_rows):
    rows, columns = kernel.shape[2:]
    width = pieces[0].shape[1]
    if adjoint:
        tile = columns // 2 if columns % 256 == 0 and columns > 640 else columns
        steps, shape, given, made = columns // tile, (2, 1, rows, tile), rows, columns
        k_spec = pl.BlockSpec(shape, lambda i: (0, slab, 0, i))
    else:
        tile = rows // 4
        steps, shape, given, made = rows // tile, (2, 1, tile, columns), columns, rows
        k_spec = pl.BlockSpec(shape, lambda i: (0, slab, i, 0))
    shapes = [
        ((len(out),) if len(out) > 1 else ()) + (out_rows + HEAD, width) for out in outs
    ]
    return pl.pallas_call(
        functools.partial(product_kernel, adjoint, places, outs),
        grid=(steps,),
        in_specs=[k_spec] + [pl.BlockSpec(p.shape, lambda i: (0, 0)) for p in pieces],
        out_specs=[pl.BlockSpec(s, lambda i, n=len(s): (0,) * n) for s in shapes],
        out_shape=[jax.ShapeDtypeStruct(s, jnp.float32) for s in shapes],
        scratch_shapes=[
            pltpu.VMEM((HEAD, width), jnp.float32),
            pltpu.VMEM((given, width), jnp.bfloat16),
            pltpu.VMEM((given, width), jnp.bfloat16),
            pltpu.VMEM((made, width), jnp.float32),
        ],
        compiler_params=pltpu.CompilerParams(vmem_limit_bytes=VMEM_BYTES),
        cost_estimate=pl.CostEstimate(
            flops=2 * 3 * 2 * rows * columns * width,
            bytes_accessed=8 * rows * columns + 4 * width * (rows + columns),
            transcendentals=0,
        ),
    )(kernel, *pieces)


def finish_kernel(count, parts, *refs):
    part_refs, refs = refs[:parts], refs[parts:]
    piece_ref, norm_ref = refs[-2:]
    total = part_refs[0][...]
    for part in part_refs[1:]:
        total = total + part[...]
    norm = jnp.sqrt(total[:1, :1] / count)
    data = total[HEAD:, :] / norm
    if len(refs) > 2:
        other, last_norm = refs[:2]
        data = data - norm * (other[HEAD:, :] / last_norm[:1, :1])
    piece_ref[HEAD:, :] = data
    piece_ref[:HEAD, :] = jnp.broadcast_to(jnp.sum(data * data), (HEAD, data.shape[1]))
    norm_ref[...] = jnp.broadcast_to(norm, norm_ref.shape)


def finish(count, parts, *other):
    shape = parts[0].shape
    return pl.pallas_call(
        functools.partial(finish_kernel, count, len(parts)),
        out_shape=[
            jax.ShapeDtypeStruct(shape, jnp.float32),
            jax.ShapeDtypeStruct((8, 128), jnp.float32),
        ],
        compiler_params=pltpu.CompilerParams(vmem_limit_bytes=VMEM_BYTES),
        cost_estimate=pl.CostEstimate(
            flops=shape[0] * shape[1] * 8,
            bytes_accessed=4 * shape[0] * shape[1] * (len(parts) + 2),
            transcendentals=0,
        ),
    )(*parts, *other)


def pack_kernel(place_ref, mark_ref, traces_ref, first_ref, second_ref):
    slots = first_ref.shape[0]
    spots = lax.broadcasted_iota(jnp.int32, (place_ref.shape[0], slots), 1)
    chosen = (place_ref[...] == spots).astype(jnp.bfloat16)
    width = second_ref.shape[1]
    half = width // 2
    packed = dot_exact(chosen, traces_ref[...])
    marks = jnp.broadcast_to(mark_ref[...], (mark_ref.shape[0], 128))
    first_ref[:, :half] = packed[:, :half]
    first_ref[:, half:width] = packed[:, width : width + half]
    first_ref[:, width:] = dot_exact(chosen, marks)
    second_ref[:, :half] = packed[:, half:width]
    second_ref[:, half:] = packed[:, width + half :]


def unpack_kernel(data_ref, mark_ref, piece_ref):
    rows = piece_ref.shape[0] - HEAD
    width = piece_ref.shape[1]
    slots = data_ref.shape[0]
    spots = lax.broadcasted_iota(jnp.int32, (slots, rows), 1) + 1
    chosen = (mark_ref[:, :1].astype(jnp.int32) == spots).astype(jnp.bfloat16)
    data = dot_exact(chosen, data_ref[:, :width])
    piece_ref[HEAD:, :] = data
    piece_ref[:HEAD, :] = jnp.broadcast_to(jnp.sum(data * data), (HEAD, width))


def dispatch(traces, acq_lists, counts, row_count):
    areas = lax.axis_size("z") * lax.axis_size("y")
    slot_count = traces.shape[1]
    width = traces.shape[2] * traces.shape[4]
    peer = -(-slot_count // areas)
    ids = acq_lists[0]
    slot_iota = jnp.arange(slot_count, dtype=jnp.int32)
    area = jnp.where(slot_iota < counts[0, 0], ids // row_count, -1)
    before = (area[:, None] == area[None, :]) & (slot_iota[None, :] < slot_iota[:, None])
    rank = jnp.sum(before.astype(jnp.int32), axis=1)
    place = jnp.where(area >= 0, area * peer + rank, -1)
    mark = (ids % row_count + 1).astype(jnp.float32)
    params = pltpu.CompilerParams(vmem_limit_bytes=VMEM_BYTES)
    slots = areas * peer
    first, second = pl.pallas_call(
        pack_kernel,
        out_shape=[
            jax.ShapeDtypeStruct((slots, width + 128), jnp.float32),
            jax.ShapeDtypeStruct((slots, width), jnp.float32),
        ],
        compiler_params=params,
    )(place[:, None], mark[:, None], traces.reshape(slot_count, -1))

    def exchange(packed):
        packed = packed.reshape(areas, peer, -1)
        packed = lax.all_to_all(packed, REC, 0, 0, tiled=True)
        return packed.reshape(slots, -1)

    unpack = pl.pallas_call(
        unpack_kernel,
        out_shape=jax.ShapeDtypeStruct((row_count + HEAD, width), jnp.float32),
        compiler_params=params,
    )
    return [first, second], exchange, unpack


def swap(values, axis, k=1):
    size = lax.axis_size(axis)
    return lax.ppermute(values, axis, [(i, i ^ k) for i in range(size)])


def at_end():
    index = lax.axis_index("z")
    return (index == 0) | (index == 3)


ASKED = {
    "y": lambda values: swap(values, "y"),
    "x": lambda values: swap(values, "x"),
    "c": lambda values: swap(values, "c"),
    "z": lambda values: swap(values, "z"),
    "mid": lambda values: lax.ppermute(values, "z", [(1, 2), (2, 1)]),
    "up": lambda values: lax.ppermute(values, "z", [(0, 1), (3, 2)]),
    "down": lambda values: lax.ppermute(values, "z", [(1, 0), (2, 3)]),
    "hold": lambda values: values,
}


def answer(asked):
    results = [None] * len(asked)
    kinds = [kind for kind, _ in asked]
    if "up" in kinds and "down" in kinds:
        up, down = kinds.index("up"), kinds.index("down")
        both = jnp.where(at_end(), asked[up][1], asked[down][1])
        results[up] = results[down] = swap(both, "z")
    for kind in ASKED:
        for index, (wanted, values) in enumerate(asked):
            if wanted == kind and results[index] is None:
                results[index] = ASKED[kind](values)
    for index, (wanted, values) in enumerate(asked):
        if results[index] is None:
            results[index] = swap(values, *wanted)
    return results


def line_place(kind):
    index = lax.axis_index("z")
    if kind == "own":
        return index
    if kind == "partner":
        return other("z")
    near = jnp.where(index < 2, 1, 0)
    return 1 + near if kind == "third" else 3 * near


def rec_place(kind, across):
    return lambda: line_place(kind) * 2 + (other("y") if across else lax.axis_index("y"))


def src_place(across_x, across_c):
    return lambda: (other("x") if across_x else lax.axis_index("x")) * 2 + (
        other("c") if across_c else lax.axis_index("c")
    )


KINDS = ("own", "partner", "third", "far")


class Neighbours:
    rec_outs = [[rec_place(kind, across)] for across in (0, 1) for kind in KINDS]
    src_outs = [[src_place(0, 1), src_place(1, 1)], [src_place(1, 0)], [src_place(0, 0)]]

    def gather_src(self, own):
        x, c = yield ("x", own), ("c", own)
        return [own, x, c, swap(x, "c")], [src_place(*k) for k in ((0, 0), (1, 0), (0, 1), (1, 1))]

    def gather_rec(self, own):
        own_y, partner, mid = yield ("y", own), ("z", own), ("mid", own)
        third, mid_two, own_y = yield ("down", mid), ("mid", partner), ("hold", own_y)
        third = jnp.where(at_end(), third, mid)
        third_y, far, own_y = yield ("y", third), ("down", mid_two), ("hold", own_y)
        far = jnp.where(at_end(), far, mid_two)
        far_y, partner_y, third_y = yield ("y", far), ("z", own_y), ("hold", third_y)
        return [own, partner, third, far, own_y, partner_y, third_y, far_y], [
            place for (place,) in self.rec_outs
        ]

    def scatter_rec(self, blocks):
        blocks = yield tuple(("hold", block) for block in blocks)
        own, partner, third, far, own_y, partner_y, third_y, far_y = blocks
        got_far, got_own_y, third_y, own_y, third = yield (
            ("y", far_y), ("z", partner_y), ("hold", third_y), ("hold", own_y), ("hold", third),
        )
        own_y = own_y + got_own_y
        far = far + got_far
        got_third, got_far, own_y, third, far = yield (
            ("y", third_y), ("up", far), ("hold", own_y), ("hold", third), ("hold", far),
        )
        third = third + got_third
        far = far + got_far
        got_third, got_partner, own_y, third = yield (
            ("up", third), ("mid", far), ("hold", own_y), ("hold", third),
        )
        partner = partner + got_partner
        third = third + got_third
        last = yield ("y", own_y), ("z", partner), ("mid", third)
        return [own, *last]

    def scatter_src(self, blocks):
        sent, across, own = yield tuple(("hold", block) for block in blocks)
        back = swap(sent, "c")
        (far,) = yield (("x", across + back[1]),)
        return [own, back[0], far]


class Whole:
    rec_outs = [[None]]
    src_outs = [[None]]

    def gather(self, piece, axes):
        pieces = lax.all_gather(piece, axes, axis=0, tiled=False)
        data = pieces[:, HEAD:].reshape(-1, piece.shape[1])
        return [jnp.concatenate([jnp.sum(pieces[:, :HEAD], axis=0), data], axis=0)], [None]

    def scatter(self, blocks, axes):
        count = lax.axis_size(axes[0]) * lax.axis_size(axes[1])
        width = blocks[0].shape[1]
        head = jnp.broadcast_to(blocks[0][:HEAD], (count, HEAD, width))
        data = blocks[0][HEAD:].reshape(count, -1, width)
        both = jnp.concatenate([head, data], axis=1)
        return [lax.psum_scatter(both, axes, scatter_dimension=0, tiled=False)]

    def gather_src(self, piece):
        (piece,) = yield (("hold", piece),)
        return self.gather(piece, SRC)

    def gather_rec(self, piece):
        (piece,) = yield (("hold", piece),)
        return self.gather(piece, REC)

    def scatter_rec(self, blocks):
        (blocks,) = yield (("hold", blocks),)
        return self.scatter(blocks, REC)

    def scatter_src(self, blocks):
        (blocks,) = yield (("hold", blocks),)
        return self.scatter(blocks, SRC)


def global_sum(values):
    for axis in ("c", "x", "y", "z"):
        k = 1
        while k < lax.axis_size(axis):
            (got,) = yield (((axis, 2 * k - 1), values),)
            values = values + got
            k *= 2
    return values


LAG = 4


def in_slots(chains, lag):
    values, results, slot = [None] * len(chains), [None] * len(chains), 0
    live = list(range(len(chains)))
    while live:
        made = {}
        for index in list(live):
            if slot < index * lag:
                continue
            try:
                made[index] = chains[index].send(values[index])
            except StopIteration as stop:
                results[index] = stop.value
                live.remove(index)
        asked = [request for requests in made.values() for request in requests]
        given = iter(lax.optimization_barrier(tuple(answer(asked))))
        for index, requests in made.items():
            values[index] = tuple(next(given) for _ in requests)
        slot += 1
    return results


def chain(moves, kernel, slab, packed, shared, exchange, unpack, row_count, column_count, count):
    def adjoint(piece):
        pieces, places = yield from moves.gather_src(piece)
        rows = column_count if len(moves.rec_outs) > 1 else kernel.shape[3]
        blocks = product(kernel, slab, True, pieces, places, moves.rec_outs, rows)
        return (yield from moves.scatter_rec(blocks))

    def forward(piece):
        pieces, places = yield from moves.gather_rec(piece)
        rows = row_count if len(moves.src_outs) > 1 else kernel.shape[2]
        blocks = product(kernel, slab, False, pieces, places, moves.src_outs, rows)
        return (yield from moves.scatter_src(blocks))

    (packed,) = yield (("hold", packed),)
    (packed,) = yield (("hold", exchange(packed)),)
    if slab == 0:
        shared["marks"] = packed[:, 2 * SOURCES :]
    left = unpack(packed, shared["marks"])
    right, beta = finish(count, (yield from adjoint(left)))
    rights, norms = [], [beta]
    for iteration in range(ITERS):
        left, alpha = finish(count, (yield from forward(right)), left, beta)
        rights.append(right)
        norms.append(alpha)
        if iteration + 1 < ITERS:
            right, beta = finish(count, (yield from adjoint(left)), right, alpha)
            norms.append(beta)
    norms.append((yield from global_sum(left[:HEAD, :128])))
    return rights, norms, left


def join_left_kernel(*refs):
    out = refs[-1]
    half = refs[0].shape[1] // 2
    for slab, left in enumerate(refs[:-1]):
        for part in range(2):
            at = (part * FREQS + slab) * half
            out[:, at : at + half] = left[HEAD:, part * half : (part + 1) * half]


def join_solution_kernel(count, *refs):
    refs, out = refs[:-1], refs[-1]
    half = refs[0].shape[1] // 2
    for slab in range(FREQS):
        start = slab * (3 * ITERS + 1)
        rights = refs[start : start + ITERS]
        norms = [ref[:1, :1] for ref in refs[start + ITERS : start + 3 * ITERS + 1]]
        norms[-1] = jnp.sqrt(norms[-1] / count)
        phibar, betas, alphas = norms[0], norms[2::2], norms[1::2]
        for iteration in range(ITERS):
            unit = rights[iteration][HEAD:, :] / alphas[iteration]
            if iteration == 0:
                rhobar, search = alphas[0], unit
            else:
                rhobar = -cosine * alphas[iteration]
                search = unit - (sine * alphas[iteration] / rho) * search
            rho = jnp.sqrt(rhobar * rhobar + betas[iteration] * betas[iteration])
            cosine = rhobar / rho
            sine = betas[iteration] / rho
            phi = cosine * phibar
            phibar = sine * phibar
            step = (phi / rho) * search
            solution = step if iteration == 0 else solution + step
        for part in range(2):
            at = (part * FREQS + slab) * half
            out[:, at : at + half] = solution[:, part * half : (part + 1) * half]


def join(kernel, pieces):
    rows, width = pieces[0].shape[0] - HEAD, pieces[0].shape[1] * FREQS
    joined = pl.pallas_call(
        kernel,
        out_shape=jax.ShapeDtypeStruct((rows, width), jnp.float32),
        compiler_params=pltpu.CompilerParams(vmem_limit_bytes=VMEM_BYTES),
        cost_estimate=pl.CostEstimate(
            flops=rows * width * 4, bytes_accessed=8 * rows * width, transcendentals=0
        ),
    )(*pieces)
    return joined.reshape(rows, 2, FREQS, SOURCES)


def on_device(kernel, traces, acq_lists, counts):
    sizes = tuple(lax.axis_size(axis) for axis in ("z", "y", "x", "c"))
    row_count = kernel.shape[2] // (sizes[2] * sizes[3])
    column_count = kernel.shape[3] // (sizes[0] * sizes[1])
    aligned = row_count % 16 == 0 and column_count % 16 == 0
    moves = Neighbours() if sizes == (4, 2, 2, 2) and aligned else Whole()
    count = 2.0 * kernel.shape[2] * sizes[0] * sizes[1] * SOURCES
    shared = {}
    packed, exchange, unpack = dispatch(traces, acq_lists, counts, row_count)
    chains = [
        chain(
            moves, kernel, slab, packed[slab], shared, exchange, unpack,
            row_count, column_count, count,
        )
        for slab in range(FREQS)
    ]
    rights, norms, lefts = zip(*in_slots(chains, LAG))
    given = [ref for pair in zip(rights, norms) for group in pair for ref in group]
    return join(functools.partial(join_solution_kernel, count), given), join(
        join_left_kernel, lefts
    )


def solution(mesh):
    rec, src = mesh.shape["rec"], mesh.shape["src"]
    depth = src // 2
    fine = Mesh(
        mesh.devices.reshape(rec // depth, depth, depth, 2), REC + SRC
    )
    placed = (
        P(None, None, REC, SRC),
        P(SRC, REC, None, None, None),
        P(SRC, REC),
        P(SRC, REC),
    )
    return jax.shard_map(
        on_device,
        mesh=fine,
        in_specs=placed,
        out_specs=(P(SRC + REC, None, None, None), P(REC + SRC, None, None, None)),
        check_vma=False,
    )
```

```python
import functools
import jax
import jax.numpy as jnp
from jax import lax
from jax.experimental import pallas as pl
from jax.experimental.pallas import tpu as pltpu
from jax.sharding import Mesh, PartitionSpec as P

FREQS = 2
SOURCES = 256
ITERS = 2
LANES = 128
HEAD = 8
CHUNKS = 2 * SOURCES // LANES
REC = ("z", "y")
SRC = ("x", "c")
VMEM_BYTES = 50 * 2**20


def split(values):
    high = values.astype(jnp.bfloat16)
    return high, (values - high.astype(jnp.float32)).astype(jnp.bfloat16)


def dot_three(left, right, dims):
    def dot(a, b):
        return lax.dot_general(a, b, (dims, ((), ())), preferred_element_type=jnp.float32)

    return dot(left[0], right[0]) + (dot(left[0], right[1]) + dot(left[1], right[0]))


def dot_exact(chosen, values):
    total = None
    for _ in range(3):
        part = values.astype(jnp.bfloat16)
        values = values - part.astype(jnp.float32)
        term = lax.dot_general(
            chosen, part, (((0,), (0,)), ((), ())), preferred_element_type=jnp.float32
        )
        total = term if total is None else total + term
    return total


def other(axis):
    index = lax.axis_index(axis)
    return index + 1 - 2 * lax.rem(index, 2)


def product_kernel(adjoint, places, outs, k_ref, *refs):
    piece_refs = refs[: len(places)]
    out_refs = refs[len(places) : len(places) + len(outs)]
    head, sum_high, sum_low, real_high, real_low, imag_high, imag_low, total = refs[
        len(places) + len(outs) :
    ]
    step = pl.program_id(0)
    half = real_high.shape[1]

    @pl.when(step == 0)
    def _():
        sums = None
        for place, piece in zip(places, piece_refs):
            rows = (piece.shape[0] - HEAD) // CHUNKS
            at = 0 if place is None else pl.multiple_of(place() * rows, rows)
            here = pl.ds(at, rows)
            for chunk in range(CHUNKS // 2):
                lanes = slice(chunk * LANES, (chunk + 1) * LANES)
                start = HEAD + chunk * rows
                real = piece[start : start + rows, :]
                start += CHUNKS // 2 * rows
                imag = piece[start : start + rows, :]
                if adjoint:
                    imag = -imag
                sum_high[here, lanes], sum_low[here, lanes] = split(real + imag)
                real_high[here, lanes], real_low[here, lanes] = split(real)
                imag_high[here, lanes], imag_low[here, lanes] = split(imag)
            sums = piece[:HEAD, :] if sums is None else sums + piece[:HEAD, :]
        head[...] = sums

    dims = ((0,), (0,)) if adjoint else ((1,), (0,))
    k_real, k_imag = k_ref[0, 0], k_ref[1, 0]
    first = dot_three(split(k_real), (sum_high[...], sum_low[...]), dims)
    second = dot_three(split(k_imag - k_real), (real_high[...], real_low[...]), dims)
    third = dot_three(split(k_real + k_imag), (imag_high[...], imag_low[...]), dims)
    rows = first.shape[0]
    at = pl.multiple_of(step * rows, rows)
    total[pl.ds(at, rows), :half] = first - third
    total[pl.ds(at, rows), half:] = -(first + second) if adjoint else first + second

    @pl.when(step == pl.num_programs(0) - 1)
    def _():
        for out, out_ref in zip(outs, out_refs):
            for slot, place in enumerate(out):
                target = out_ref.at[slot] if len(out) > 1 else out_ref
                rows = (target.shape[0] - HEAD) // CHUNKS
                at = 0 if place is None else pl.multiple_of(place() * rows, rows)
                target[:HEAD, :] = head[...]
                for chunk in range(CHUNKS):
                    lanes = slice(chunk * LANES, (chunk + 1) * LANES)
                    start = HEAD + chunk * rows
                    target[start : start + rows, :] = total[pl.ds(at, rows), lanes]


def product(kernel, slab, adjoint, pieces, places, outs, out_rows):
    rows, columns = kernel.shape[2:]
    width = 2 * SOURCES
    if adjoint:
        tile = columns // 2 if columns % 256 == 0 and columns > 640 else columns
        steps, shape, given, made = columns // tile, (2, 1, rows, tile), rows, columns
        k_spec = pl.BlockSpec(shape, lambda i: (0, slab, 0, i))
    else:
        tile = rows // 2
        steps, shape, given, made = rows // tile, (2, 1, tile, columns), columns, rows
        k_spec = pl.BlockSpec(shape, lambda i: (0, slab, i, 0))
    shapes = [
        ((len(out),) if len(out) > 1 else ()) + (HEAD + CHUNKS * out_rows, LANES) for out in outs
    ]
    return pl.pallas_call(
        functools.partial(product_kernel, adjoint, places, outs),
        grid=(steps,),
        in_specs=[k_spec] + [pl.BlockSpec(p.shape, lambda i: (0, 0)) for p in pieces],
        out_specs=[pl.BlockSpec(s, lambda i, n=len(s): (0,) * n) for s in shapes],
        out_shape=[jax.ShapeDtypeStruct(s, jnp.float32) for s in shapes],
        scratch_shapes=[pltpu.VMEM((HEAD, LANES), jnp.float32)]
        + [pltpu.VMEM((given, SOURCES), jnp.bfloat16)] * 6
        + [pltpu.VMEM((made, width), jnp.float32)],
        compiler_params=pltpu.CompilerParams(vmem_limit_bytes=VMEM_BYTES),
        cost_estimate=pl.CostEstimate(
            flops=2 * 3 * 2 * rows * columns * width,
            bytes_accessed=8 * rows * columns + 4 * width * (rows + columns),
            transcendentals=0,
        ),
    )(kernel, *pieces)


def finish_kernel(count, parts, *refs):
    part_refs, refs = refs[:parts], refs[parts:]
    piece_ref, norm_ref = refs[-2:]
    total = part_refs[0][...]
    for part in part_refs[1:]:
        total = total + part[...]
    norm = jnp.sqrt(total[:1, :1] / count)
    data = total[HEAD:, :] / norm
    if len(refs) > 2:
        other, last_norm = refs[:2]
        data = data - norm * (other[HEAD:, :] / last_norm[:1, :1])
    piece_ref[HEAD:, :] = data
    piece_ref[:HEAD, :] = jnp.broadcast_to(jnp.sum(data * data), (HEAD, data.shape[1]))
    norm_ref[...] = jnp.broadcast_to(norm, norm_ref.shape)


def finish(count, parts, *other):
    shape = parts[0].shape
    return pl.pallas_call(
        functools.partial(finish_kernel, count, len(parts)),
        out_shape=[
            jax.ShapeDtypeStruct(shape, jnp.float32),
            jax.ShapeDtypeStruct((8, 128), jnp.float32),
        ],
        compiler_params=pltpu.CompilerParams(vmem_limit_bytes=VMEM_BYTES),
        cost_estimate=pl.CostEstimate(
            flops=shape[0] * shape[1] * 8,
            bytes_accessed=4 * shape[0] * shape[1] * (len(parts) + 2),
            transcendentals=0,
        ),
    )(*parts, *other)


def pack_kernel(place_ref, mark_ref, traces_ref, first_ref, second_ref):
    slots = first_ref.shape[0]
    spots = lax.broadcasted_iota(jnp.int32, (place_ref.shape[0], slots), 1)
    chosen = (place_ref[...] == spots).astype(jnp.bfloat16)
    width = second_ref.shape[1]
    half = width // 2
    packed = dot_exact(chosen, traces_ref[...])
    marks = jnp.broadcast_to(mark_ref[...], (mark_ref.shape[0], 128))
    first_ref[:, :half] = packed[:, :half]
    first_ref[:, half:width] = packed[:, width : width + half]
    first_ref[:, width:] = dot_exact(chosen, marks)
    second_ref[:, :half] = packed[:, half:width]
    second_ref[:, half:] = packed[:, width + half :]


def unpack_kernel(data_ref, mark_ref, piece_ref):
    rows = (piece_ref.shape[0] - HEAD) // CHUNKS
    width = 2 * SOURCES
    slots = data_ref.shape[0]
    spots = lax.broadcasted_iota(jnp.int32, (slots, rows), 1) + 1
    chosen = (mark_ref[:, :1].astype(jnp.int32) == spots).astype(jnp.bfloat16)
    data = dot_exact(chosen, data_ref[:, :width])
    for chunk in range(CHUNKS):
        start = HEAD + chunk * rows
        piece_ref[start : start + rows, :] = data[:, chunk * LANES : (chunk + 1) * LANES]
    piece_ref[:HEAD, :] = jnp.broadcast_to(jnp.sum(data * data), (HEAD, LANES))


def dispatch(traces, acq_lists, counts, row_count):
    areas = lax.axis_size("z") * lax.axis_size("y")
    slot_count = traces.shape[1]
    width = traces.shape[2] * traces.shape[4]
    peer = -(-slot_count // areas)
    ids = acq_lists[0]
    slot_iota = jnp.arange(slot_count, dtype=jnp.int32)
    area = jnp.where(slot_iota < counts[0, 0], ids // row_count, -1)
    before = (area[:, None] == area[None, :]) & (slot_iota[None, :] < slot_iota[:, None])
    rank = jnp.sum(before.astype(jnp.int32), axis=1)
    place = jnp.where(area >= 0, area * peer + rank, -1)
    mark = (ids % row_count + 1).astype(jnp.float32)
    params = pltpu.CompilerParams(vmem_limit_bytes=VMEM_BYTES)
    slots = areas * peer
    first, second = pl.pallas_call(
        pack_kernel,
        out_shape=[
            jax.ShapeDtypeStruct((slots, width + 128), jnp.float32),
            jax.ShapeDtypeStruct((slots, width), jnp.float32),
        ],
        compiler_params=params,
    )(place[:, None], mark[:, None], traces.reshape(slot_count, -1))

    def exchange(packed):
        packed = packed.reshape(areas, peer, -1)
        packed = lax.all_to_all(packed, REC, 0, 0, tiled=True)
        return packed.reshape(slots, -1)

    unpack = pl.pallas_call(
        unpack_kernel,
        out_shape=jax.ShapeDtypeStruct((HEAD + CHUNKS * row_count, LANES), jnp.float32),
        compiler_params=params,
    )
    return [first, second], exchange, unpack


def swap(values, axis, k=1):
    size = lax.axis_size(axis)
    return lax.ppermute(values, axis, [(i, i ^ k) for i in range(size)])


def at_end():
    index = lax.axis_index("z")
    return (index == 0) | (index == 3)


ASKED = {
    "y": lambda values: swap(values, "y"),
    "x": lambda values: swap(values, "x"),
    "c": lambda values: swap(values, "c"),
    "z": lambda values: swap(values, "z"),
    "mid": lambda values: lax.ppermute(values, "z", [(1, 2), (2, 1)]),
    "up": lambda values: swap(values, "z"),
    "down": lambda values: swap(values, "z"),
    "hold": lambda values: values,
}


def answer(asked):
    results = [None] * len(asked)
    kinds = [kind for kind, _ in asked]
    if "up" in kinds and "down" in kinds:
        up, down = kinds.index("up"), kinds.index("down")
        both = jnp.where(at_end(), asked[up][1], asked[down][1])
        results[up] = results[down] = swap(both, "z")
    for kind in ASKED:
        for index, (wanted, values) in enumerate(asked):
            if wanted == kind and results[index] is None:
                results[index] = ASKED[kind](values)
    for index, (wanted, values) in enumerate(asked):
        if results[index] is None:
            results[index] = swap(values, *wanted)
    return results


def line_place(kind):
    index = lax.axis_index("z")
    if kind == "own":
        return index
    if kind == "partner":
        return other("z")
    near = jnp.where(index < 2, 1, 0)
    return 1 + near if kind == "third" else 3 * near


def rec_place(kind, across):
    return lambda: line_place(kind) * 2 + (other("y") if across else lax.axis_index("y"))


def src_place(across_x, across_c):
    return lambda: (other("x") if across_x else lax.axis_index("x")) * 2 + (
        other("c") if across_c else lax.axis_index("c")
    )


KINDS = ("own", "partner", "third", "far")


class Neighbours:
    rec_outs = [[rec_place(kind, across)] for across in (0, 1) for kind in KINDS]
    src_outs = [[src_place(0, 1), src_place(1, 1)], [src_place(1, 0)], [src_place(0, 0)]]

    def gather_src(self, own):
        x, c = yield ("x", own), ("c", own)
        return [own, x, c, swap(x, "c")], [src_place(*k) for k in ((0, 0), (1, 0), (0, 1), (1, 1))]

    def gather_rec(self, own):
        own_y, partner, mid = yield ("y", own), ("z", own), ("mid", own)
        third, mid_two, own_y = yield ("down", mid), ("mid", partner), ("hold", own_y)
        third = jnp.where(at_end(), third, mid)
        third_y, far, own_y = yield ("y", third), ("down", mid_two), ("hold", own_y)
        far = jnp.where(at_end(), far, mid_two)
        far_y, partner_y, third_y = yield ("y", far), ("z", own_y), ("hold", third_y)
        return [own, partner, third, far, own_y, partner_y, third_y, far_y], [
            place for (place,) in self.rec_outs
        ]

    def scatter_rec(self, blocks):
        blocks = yield tuple(("hold", block) for block in blocks)
        own, partner, third, far, own_y, partner_y, third_y, far_y = blocks
        got_far, got_own_y, third_y, own_y, third = yield (
            ("y", far_y), ("z", partner_y), ("hold", third_y), ("hold", own_y), ("hold", third),
        )
        own_y = own_y + got_own_y
        far = far + got_far
        got_third, got_far, own_y, third, far = yield (
            ("y", third_y), ("up", far), ("hold", own_y), ("hold", third), ("hold", far),
        )
        third = third + got_third
        far = far + got_far
        got_third, got_partner, own_y, third = yield (
            ("up", third), ("mid", far), ("hold", own_y), ("hold", third),
        )
        partner = partner + got_partner
        third = third + got_third
        last = yield ("y", own_y), ("z", partner), ("mid", third)
        return [own, *last]

    def scatter_src(self, blocks):
        sent, across, own = yield tuple(("hold", block) for block in blocks)
        back = swap(sent, "c")
        (far,) = yield (("x", across + back[1]),)
        return [own, back[0], far]


class Whole:
    rec_outs = [[None]]
    src_outs = [[None]]

    def gather(self, piece, axes):
        pieces = lax.all_gather(piece, axes, axis=0, tiled=False)
        data = pieces[:, HEAD:].reshape(pieces.shape[0], CHUNKS, -1, LANES)
        data = data.transpose(1, 0, 2, 3).reshape(-1, LANES)
        return [jnp.concatenate([jnp.sum(pieces[:, :HEAD], axis=0), data], axis=0)], [None]

    def scatter(self, blocks, axes):
        count = lax.axis_size(axes[0]) * lax.axis_size(axes[1])
        head = jnp.broadcast_to(blocks[0][:HEAD], (count, HEAD, LANES))
        data = blocks[0][HEAD:].reshape(CHUNKS, count, -1, LANES)
        data = data.transpose(1, 0, 2, 3).reshape(count, -1, LANES)
        both = jnp.concatenate([head, data], axis=1)
        return [lax.psum_scatter(both, axes, scatter_dimension=0, tiled=False)]

    def gather_src(self, piece):
        (piece,) = yield (("hold", piece),)
        return self.gather(piece, SRC)

    def gather_rec(self, piece):
        (piece,) = yield (("hold", piece),)
        return self.gather(piece, REC)

    def scatter_rec(self, blocks):
        (blocks,) = yield (("hold", blocks),)
        return self.scatter(blocks, REC)

    def scatter_src(self, blocks):
        (blocks,) = yield (("hold", blocks),)
        return self.scatter(blocks, SRC)


def global_sum(values):
    for axis in ("c", "x", "y", "z"):
        k = 1
        while k < lax.axis_size(axis):
            (got,) = yield (((axis, 2 * k - 1), values),)
            values = values + got
            k *= 2
    return values


LAG = 4


def in_slots(chains, lag):
    values, results, slot = [None] * len(chains), [None] * len(chains), 0
    live = list(range(len(chains)))
    while live:
        made = {}
        for index in list(live):
            if slot < index * lag:
                continue
            try:
                made[index] = chains[index].send(values[index])
            except StopIteration as stop:
                results[index] = stop.value
                live.remove(index)
        asked = [request for requests in made.values() for request in requests]
        given = iter(lax.optimization_barrier(tuple(answer(asked))))
        for index, requests in made.items():
            values[index] = tuple(next(given) for _ in requests)
        slot += 1
    return results


def chain(moves, kernel, slab, packed, shared, exchange, unpack, row_count, column_count, count):
    def adjoint(piece):
        pieces, places = yield from moves.gather_src(piece)
        rows = column_count if len(moves.rec_outs) > 1 else kernel.shape[3]
        blocks = product(kernel, slab, True, pieces, places, moves.rec_outs, rows)
        return (yield from moves.scatter_rec(blocks))

    def forward(piece):
        pieces, places = yield from moves.gather_rec(piece)
        rows = row_count if len(moves.src_outs) > 1 else kernel.shape[2]
        blocks = product(kernel, slab, False, pieces, places, moves.src_outs, rows)
        return (yield from moves.scatter_src(blocks))

    (packed,) = yield (("hold", exchange(packed)),)
    if slab == 0:
        shared["marks"] = packed[:, 2 * SOURCES :]
    left = unpack(packed, shared["marks"])
    right, beta = finish(count, (yield from adjoint(left)))
    rights, norms = [], [beta]
    for iteration in range(ITERS):
        left, alpha = finish(count, (yield from forward(right)), left, beta)
        rights.append(right)
        norms.append(alpha)
        if iteration + 1 < ITERS:
            right, beta = finish(count, (yield from adjoint(left)), right, alpha)
            norms.append(beta)
    norms.append((yield from global_sum(left[:HEAD])))
    return rights, norms, left


def put_slab(out, slab, piece):
    rows, each = out.shape[0], CHUNKS // 2
    for chunk in range(CHUNKS):
        at = (chunk // each * FREQS + slab) * SOURCES + chunk % each * LANES
        out[:, at : at + LANES] = piece[chunk * rows : (chunk + 1) * rows, :]


def join_left_kernel(*refs):
    for slab, left in enumerate(refs[:-1]):
        put_slab(refs[-1], slab, left[HEAD:, :])


def join_solution_kernel(count, *refs):
    refs, out = refs[:-1], refs[-1]
    for slab in range(FREQS):
        start = slab * (3 * ITERS + 1)
        rights = refs[start : start + ITERS]
        norms = [ref[:1, :1] for ref in refs[start + ITERS : start + 3 * ITERS + 1]]
        norms[-1] = jnp.sqrt(norms[-1] / count)
        phibar, betas, alphas = norms[0], norms[2::2], norms[1::2]
        for iteration in range(ITERS):
            unit = rights[iteration][HEAD:, :] / alphas[iteration]
            if iteration == 0:
                rhobar, search = alphas[0], unit
            else:
                rhobar = -cosine * alphas[iteration]
                search = unit - (sine * alphas[iteration] / rho) * search
            rho = jnp.sqrt(rhobar * rhobar + betas[iteration] * betas[iteration])
            cosine = rhobar / rho
            sine = betas[iteration] / rho
            phi = cosine * phibar
            phibar = sine * phibar
            step = (phi / rho) * search
            solution = step if iteration == 0 else solution + step
        put_slab(out, slab, solution)


def join(kernel, pieces):
    rows, width = (pieces[0].shape[0] - HEAD) // CHUNKS, 2 * FREQS * SOURCES
    joined = pl.pallas_call(
        kernel,
        out_shape=jax.ShapeDtypeStruct((rows, width), jnp.float32),
        compiler_params=pltpu.CompilerParams(vmem_limit_bytes=VMEM_BYTES),
        cost_estimate=pl.CostEstimate(
            flops=rows * width * 4, bytes_accessed=8 * rows * width, transcendentals=0
        ),
    )(*pieces)
    return joined.reshape(rows, 2, FREQS, SOURCES)


def on_device(kernel, traces, acq_lists, counts):
    sizes = tuple(lax.axis_size(axis) for axis in ("z", "y", "x", "c"))
    row_count = kernel.shape[2] // (sizes[2] * sizes[3])
    column_count = kernel.shape[3] // (sizes[0] * sizes[1])
    aligned = row_count % 16 == 0 and column_count % 16 == 0
    moves = Neighbours() if sizes == (4, 2, 2, 2) and aligned else Whole()
    count = 2.0 * kernel.shape[2] * sizes[0] * sizes[1] * SOURCES
    shared = {}
    packed, exchange, unpack = dispatch(traces, acq_lists, counts, row_count)
    chains = [
        chain(
            moves, kernel, slab, packed[slab], shared, exchange, unpack,
            row_count, column_count, count,
        )
        for slab in range(FREQS)
    ]
    rights, norms, lefts = zip(*in_slots(chains, LAG))
    given = [ref for pair in zip(rights, norms) for group in pair for ref in group]
    return join(functools.partial(join_solution_kernel, count), given), join(
        join_left_kernel, lefts
    )


def solution(mesh):
    rec, src = mesh.shape["rec"], mesh.shape["src"]
    depth = src // 2
    fine = Mesh(
        mesh.devices.reshape(rec // depth, depth, depth, 2), REC + SRC
    )
    placed = (
        P(None, None, REC, SRC),
        P(SRC, REC, None, None, None),
        P(SRC, REC),
        P(SRC, REC),
    )
    return jax.shard_map(
        on_device,
        mesh=fine,
        in_specs=placed,
        out_specs=(P(SRC + REC, None, None, None), P(REC + SRC, None, None, None)),
        check_vma=False,
    )
```

```python
import functools
import jax
import jax.numpy as jnp
from jax import lax
from jax.experimental import pallas as pl
from jax.experimental.pallas import tpu as pltpu
from jax.sharding import Mesh, PartitionSpec as P

FREQS = 2
SOURCES = 256
ITERS = 2
LANES = 128
HEAD = 8
CHUNKS = 2 * SOURCES // LANES
REC = ("z", "y")
SRC = ("x", "c")
VMEM_BYTES = 42 * 2**20
SMALL_VMEM_BYTES = 12 * 2**20


def split(values):
    high = values.astype(jnp.bfloat16)
    return high, (values - high.astype(jnp.float32)).astype(jnp.bfloat16)


def dot_three(left, right, dims):
    def dot(a, b):
        return lax.dot_general(a, b, (dims, ((), ())), preferred_element_type=jnp.float32)

    return dot(left[0], right[0]) + (dot(left[0], right[1]) + dot(left[1], right[0]))


def dot_exact(chosen, values):
    total = None
    for _ in range(3):
        part = values.astype(jnp.bfloat16)
        values = values - part.astype(jnp.float32)
        term = lax.dot_general(
            chosen, part, (((0,), (0,)), ((), ())), preferred_element_type=jnp.float32
        )
        total = term if total is None else total + term
    return total


def other(axis):
    index = lax.axis_index(axis)
    return index + 1 - 2 * lax.rem(index, 2)


def product_kernel(adjoint, places, outs, k_ref, *refs):
    piece_refs = refs[: len(places)]
    out_refs = refs[len(places) : len(places) + len(outs)]
    head, sum_high, sum_low, real_high, real_low, imag_high, imag_low, total = refs[
        len(places) + len(outs) :
    ]
    step = pl.program_id(0)
    half = real_high.shape[1]

    @pl.when(step == 0)
    def _():
        sums = None
        for place, piece in zip(places, piece_refs):
            rows = (piece.shape[0] - HEAD) // CHUNKS
            at = 0 if place is None else pl.multiple_of(place() * rows, rows)
            here = pl.ds(at, rows)
            for chunk in range(CHUNKS // 2):
                lanes = slice(chunk * LANES, (chunk + 1) * LANES)
                start = HEAD + chunk * rows
                real = piece[start : start + rows, :]
                start += CHUNKS // 2 * rows
                imag = piece[start : start + rows, :]
                if adjoint:
                    imag = -imag
                sum_high[here, lanes], sum_low[here, lanes] = split(real + imag)
                real_high[here, lanes], real_low[here, lanes] = split(real)
                imag_high[here, lanes], imag_low[here, lanes] = split(imag)
            sums = piece[:HEAD, :] if sums is None else sums + piece[:HEAD, :]
        head[...] = sums

    dims = ((0,), (0,)) if adjoint else ((1,), (0,))
    k_real, k_imag = k_ref[0, 0], k_ref[1, 0]
    first = dot_three(split(k_real), (sum_high[...], sum_low[...]), dims)
    second = dot_three(split(k_imag - k_real), (real_high[...], real_low[...]), dims)
    third = dot_three(split(k_real + k_imag), (imag_high[...], imag_low[...]), dims)
    rows = first.shape[0]
    at = pl.multiple_of(step * rows, rows)
    total[pl.ds(at, rows), :half] = first - third
    total[pl.ds(at, rows), half:] = -(first + second) if adjoint else first + second

    @pl.when(step == pl.num_programs(0) - 1)
    def _():
        for out, out_ref in zip(outs, out_refs):
            for slot, place in enumerate(out):
                target = out_ref.at[slot] if len(out) > 1 else out_ref
                rows = (target.shape[0] - HEAD) // CHUNKS
                at = 0 if place is None else pl.multiple_of(place() * rows, rows)
                target[:HEAD, :] = head[...]
                for chunk in range(CHUNKS):
                    lanes = slice(chunk * LANES, (chunk + 1) * LANES)
                    start = HEAD + chunk * rows
                    target[start : start + rows, :] = total[pl.ds(at, rows), lanes]


def product(kernel, slab, adjoint, pieces, places, outs, out_rows):
    rows, columns = kernel.shape[2:]
    width = 2 * SOURCES
    if adjoint:
        tile = columns // 2 if columns % 256 == 0 and columns > 640 else columns
        steps, shape, given, made = columns // tile, (2, 1, rows, tile), rows, columns
        k_spec = pl.BlockSpec(shape, lambda i: (0, slab, 0, i))
    else:
        tile = rows // 2
        steps, shape, given, made = rows // tile, (2, 1, tile, columns), columns, rows
        k_spec = pl.BlockSpec(shape, lambda i: (0, slab, i, 0))
    shapes = [
        ((len(out),) if len(out) > 1 else ()) + (HEAD + CHUNKS * out_rows, LANES) for out in outs
    ]
    return pl.pallas_call(
        functools.partial(product_kernel, adjoint, places, outs),
        grid=(steps,),
        in_specs=[k_spec] + [pl.BlockSpec(p.shape, lambda i: (0, 0)) for p in pieces],
        out_specs=[pl.BlockSpec(s, lambda i, n=len(s): (0,) * n) for s in shapes],
        out_shape=[jax.ShapeDtypeStruct(s, jnp.float32) for s in shapes],
        scratch_shapes=[pltpu.VMEM((HEAD, LANES), jnp.float32)]
        + [pltpu.VMEM((given, SOURCES), jnp.bfloat16)] * 6
        + [pltpu.VMEM((made, width), jnp.float32)],
        compiler_params=pltpu.CompilerParams(vmem_limit_bytes=VMEM_BYTES),
        cost_estimate=pl.CostEstimate(
            flops=2 * 3 * 2 * rows * columns * width,
            bytes_accessed=8 * rows * columns + 4 * width * (rows + columns),
            transcendentals=0,
        ),
    )(kernel, *pieces)


def finish_kernel(count, parts, *refs):
    part_refs, refs = refs[:parts], refs[parts:]
    piece_ref, norm_ref = refs[-2:]
    total = part_refs[0][...]
    for part in part_refs[1:]:
        total = total + part[...]
    norm = jnp.sqrt(total[:1, :1] / count)
    data = total[HEAD:, :] / norm
    if len(refs) > 2:
        other, last_norm = refs[:2]
        data = data - norm * (other[HEAD:, :] / last_norm[:1, :1])
    piece_ref[HEAD:, :] = data
    piece_ref[:HEAD, :] = jnp.broadcast_to(jnp.sum(data * data), (HEAD, data.shape[1]))
    norm_ref[...] = jnp.broadcast_to(norm, norm_ref.shape)


def finish(count, parts, *other):
    shape = parts[0].shape
    return pl.pallas_call(
        functools.partial(finish_kernel, count, len(parts)),
        out_shape=[
            jax.ShapeDtypeStruct(shape, jnp.float32),
            jax.ShapeDtypeStruct((8, 128), jnp.float32),
        ],
        compiler_params=pltpu.CompilerParams(vmem_limit_bytes=SMALL_VMEM_BYTES),
        cost_estimate=pl.CostEstimate(
            flops=shape[0] * shape[1] * 8,
            bytes_accessed=4 * shape[0] * shape[1] * (len(parts) + 2),
            transcendentals=0,
        ),
    )(*parts, *other)


def pack_kernel(place_ref, mark_ref, traces_ref, packed_ref):
    slots = packed_ref.shape[0]
    spots = lax.broadcasted_iota(jnp.int32, (place_ref.shape[0], slots), 1)
    chosen = (place_ref[...] == spots).astype(jnp.bfloat16)
    packed = dot_exact(chosen, traces_ref[...])
    marks = jnp.broadcast_to(mark_ref[...], (mark_ref.shape[0], LANES))
    for slab in range(FREQS):
        for part in range(2):
            at = (2 * slab + part) * SOURCES
            start = (part * FREQS + slab) * SOURCES
            packed_ref[:, at : at + SOURCES] = packed[:, start : start + SOURCES]
    packed_ref[:, 2 * FREQS * SOURCES :] = dot_exact(chosen, marks)


def unpack_kernel(packed_ref, *piece_refs):
    slots, width = packed_ref.shape[0], 2 * SOURCES
    rows = (piece_refs[0].shape[0] - HEAD) // CHUNKS
    spots = lax.broadcasted_iota(jnp.int32, (slots, rows), 1) + 1
    marks = packed_ref[:, FREQS * width : FREQS * width + 1]
    chosen = (marks.astype(jnp.int32) == spots).astype(jnp.bfloat16)
    for slab, piece_ref in enumerate(piece_refs):
        data = dot_exact(chosen, packed_ref[:, slab * width : (slab + 1) * width])
        for chunk in range(CHUNKS):
            start = HEAD + chunk * rows
            piece_ref[start : start + rows, :] = data[:, chunk * LANES : (chunk + 1) * LANES]
        piece_ref[:HEAD, :] = jnp.broadcast_to(jnp.sum(data * data), (HEAD, LANES))


def dispatch(traces, acq_lists, counts, row_count):
    areas = lax.axis_size("z") * lax.axis_size("y")
    slot_count = traces.shape[1]
    width = traces.shape[2] * traces.shape[4]
    peer = -(-slot_count // areas)
    ids = acq_lists[0]
    slot_iota = jnp.arange(slot_count, dtype=jnp.int32)
    area = jnp.where(slot_iota < counts[0, 0], ids // row_count, -1)
    before = (area[:, None] == area[None, :]) & (slot_iota[None, :] < slot_iota[:, None])
    rank = jnp.sum(before.astype(jnp.int32), axis=1)
    place = jnp.where(area >= 0, area * peer + rank, -1)
    mark = (ids % row_count + 1).astype(jnp.float32)
    params = pltpu.CompilerParams(vmem_limit_bytes=SMALL_VMEM_BYTES)
    slots = areas * peer
    packed = pl.pallas_call(
        pack_kernel,
        out_shape=jax.ShapeDtypeStruct((slots, FREQS * width + LANES), jnp.float32),
        compiler_params=params,
    )(place[:, None], mark[:, None], traces.reshape(slot_count, -1))
    packed = packed.reshape(areas, peer, -1)
    packed = lax.all_to_all(packed, REC, 0, 0, tiled=True).reshape(slots, -1)
    piece = jax.ShapeDtypeStruct((HEAD + CHUNKS * row_count, LANES), jnp.float32)
    return pl.pallas_call(unpack_kernel, out_shape=[piece] * FREQS, compiler_params=params)(packed)


def swap(values, axis, k=1):
    size = lax.axis_size(axis)
    return lax.ppermute(values, axis, [(i, i ^ k) for i in range(size)])


def at_end():
    index = lax.axis_index("z")
    return (index == 0) | (index == 3)


LATER = "~"
ASKED = {
    "y": lambda values: swap(values, "y"),
    "x": lambda values: swap(values, "x"),
    "c": lambda values: swap(values, "c"),
    "z": lambda values: swap(values, "z"),
    "mid": lambda values: lax.ppermute(values, "z", [(1, 2), (2, 1)]),
    "up": lambda values: swap(values, "z"),
    "down": lambda values: swap(values, "z"),
    "hold": lambda values: values,
}


def answer(asked):
    results = [None] * len(asked)
    asked = [(kind.rstrip(LATER), values) for kind, values in asked]
    kinds = [kind for kind, _ in asked]
    if "up" in kinds and "down" in kinds:
        up, down = kinds.index("up"), kinds.index("down")
        both = jnp.where(at_end(), asked[up][1], asked[down][1])
        results[up] = results[down] = swap(both, "z")
    for kind in ASKED:
        for index, (wanted, values) in enumerate(asked):
            if wanted == kind and results[index] is None:
                results[index] = ASKED[kind](values)
    return results


def line_place(kind):
    index = lax.axis_index("z")
    if kind == "own":
        return index
    if kind == "partner":
        return other("z")
    near = jnp.where(index < 2, 1, 0)
    return 1 + near if kind == "third" else 3 * near


def rec_place(kind, across):
    return lambda: line_place(kind) * 2 + (other("y") if across else lax.axis_index("y"))


def src_place(across_x, across_c):
    return lambda: (other("x") if across_x else lax.axis_index("x")) * 2 + (
        other("c") if across_c else lax.axis_index("c")
    )


KINDS = ("own", "partner", "third", "far")


class Neighbours:
    rec_outs = [[rec_place(kind, across)] for across in (0, 1) for kind in KINDS]
    src_outs = [[src_place(0, 1), src_place(1, 1)], [src_place(1, 0)], [src_place(0, 0)]]

    def gather_src(self, own):
        x, c = yield ("x", own), ("c", own)
        return [own, x, c, swap(x, "c")], [src_place(*k) for k in ((0, 0), (1, 0), (0, 1), (1, 1))]

    def gather_rec(self, own):
        own_y, partner, mid = yield ("y~", own), ("z", own), ("mid", own)
        third, mid_two, own_y = yield ("down", mid), ("mid", partner), ("hold", own_y)
        third = jnp.where(at_end(), third, mid)
        third_y, far, own_y = yield ("y", third), ("down", mid_two), ("hold", own_y)
        far = jnp.where(at_end(), far, mid_two)
        far_y, partner_y, third_y = yield ("y", far), ("z", own_y), ("hold", third_y)
        return [own, partner, third, far, own_y, partner_y, third_y, far_y], [
            place for (place,) in self.rec_outs
        ]

    def scatter_rec(self, blocks):
        blocks = yield tuple(("hold", block) for block in blocks)
        own, partner, third, far, own_y, partner_y, third_y, far_y = blocks
        got_far, got_own_y, third_y, own_y, third = yield (
            ("y", far_y), ("z~", partner_y), ("hold", third_y), ("hold", own_y), ("hold", third),
        )
        far = far + got_far
        got_third, got_far, got_own_y, own_y, third, far = yield (
            ("y", third_y), ("up", far), ("hold", got_own_y), ("hold", own_y), ("hold", third),
            ("hold", far),
        )
        own_y = own_y + got_own_y
        third = third + got_third
        far = far + got_far
        got_own, got_third, got_partner, third = yield (
            ("y~", own_y), ("up", third), ("mid", far), ("hold", third),
        )
        partner = partner + got_partner
        third = third + got_third
        last = yield ("hold", got_own), ("z", partner), ("mid", third)
        return [own, *last]

    def scatter_src(self, blocks):
        sent, across, own = yield tuple(("hold", block) for block in blocks)
        back = swap(sent, "c")
        (far,) = yield (("x", across + back[1]),)
        return [own, back[0], far]


class Whole:
    rec_outs = [[None]]
    src_outs = [[None]]

    def gather(self, piece, axes):
        pieces = lax.all_gather(piece, axes, axis=0, tiled=False)
        data = pieces[:, HEAD:].reshape(pieces.shape[0], CHUNKS, -1, LANES)
        data = data.transpose(1, 0, 2, 3).reshape(-1, LANES)
        return [jnp.concatenate([jnp.sum(pieces[:, :HEAD], axis=0), data], axis=0)], [None]

    def scatter(self, blocks, axes):
        count = lax.axis_size(axes[0]) * lax.axis_size(axes[1])
        head = jnp.broadcast_to(blocks[0][:HEAD], (count, HEAD, LANES))
        data = blocks[0][HEAD:].reshape(CHUNKS, count, -1, LANES)
        data = data.transpose(1, 0, 2, 3).reshape(count, -1, LANES)
        both = jnp.concatenate([head, data], axis=1)
        return [lax.psum_scatter(both, axes, scatter_dimension=0, tiled=False)]

    def gather_src(self, piece):
        (piece,) = yield (("hold", piece),)
        return self.gather(piece, SRC)

    def gather_rec(self, piece):
        (piece,) = yield (("hold", piece),)
        return self.gather(piece, REC)

    def scatter_rec(self, blocks):
        (blocks,) = yield (("hold", blocks),)
        return self.scatter(blocks, REC)

    def scatter_src(self, blocks):
        (blocks,) = yield (("hold", blocks),)
        return self.scatter(blocks, SRC)


def global_sum(values):
    for axis in ("c", "x", "y", "z"):
        k = 1
        while k < lax.axis_size(axis):
            values = values + swap(values, axis, 2 * k - 1)
            k *= 2
    return values


LAG = 4


def in_slots(chains, lag):
    values, results, slot = [None] * len(chains), [None] * len(chains), 0
    live = list(range(len(chains)))
    while live:
        made = {}
        for index in list(live):
            if slot < index * lag:
                continue
            try:
                made[index] = chains[index].send(values[index])
            except StopIteration as stop:
                results[index] = stop.value
                live.remove(index)
        asked = [request for requests in made.values() for request in requests]
        answers = answer(asked)
        waits = [index for index, (kind, _) in enumerate(asked) if not kind.endswith(LATER)]
        closed = lax.optimization_barrier(tuple(answers[index] for index in waits))
        for index, result in zip(waits, closed):
            answers[index] = result
        given = iter(answers)
        for index, requests in made.items():
            values[index] = tuple(next(given) for _ in requests)
        slot += 1
    return results


def chain(moves, kernel, slab, left, row_count, column_count, count):
    def adjoint(piece):
        pieces, places = yield from moves.gather_src(piece)
        rows = column_count if len(moves.rec_outs) > 1 else kernel.shape[3]
        blocks = product(kernel, slab, True, pieces, places, moves.rec_outs, rows)
        return (yield from moves.scatter_rec(blocks))

    def forward(piece):
        pieces, places = yield from moves.gather_rec(piece)
        rows = row_count if len(moves.src_outs) > 1 else kernel.shape[2]
        blocks = product(kernel, slab, False, pieces, places, moves.src_outs, rows)
        return (yield from moves.scatter_src(blocks))

    right, beta = finish(count, (yield from adjoint(left)))
    rights, norms = [], [beta]
    for iteration in range(ITERS):
        left, alpha = finish(count, (yield from forward(right)), left, beta)
        rights.append(right)
        norms.append(alpha)
        if iteration + 1 < ITERS:
            right, beta = finish(count, (yield from adjoint(left)), right, alpha)
            norms.append(beta)
    return rights, norms, left


def put_slab(out, slab, piece):
    rows, each = out.shape[0], CHUNKS // 2
    for chunk in range(CHUNKS):
        at = (chunk // each * FREQS + slab) * SOURCES + chunk % each * LANES
        out[:, at : at + LANES] = piece[chunk * rows : (chunk + 1) * rows, :]


def join_left_kernel(*refs):
    for slab, left in enumerate(refs[:-1]):
        put_slab(refs[-1], slab, left[HEAD:, :])


def join_solution_kernel(count, *refs):
    refs, out = refs[:-1], refs[-1]
    for slab in range(FREQS):
        start = slab * 3 * ITERS
        rights = refs[start : start + ITERS]
        norms = [ref[:1, :1] for ref in refs[start + ITERS : start + 3 * ITERS]]
        norms.append(jnp.sqrt(refs[-1][slab : slab + 1, :1] / count))
        phibar, betas, alphas = norms[0], norms[2::2], norms[1::2]
        for iteration in range(ITERS):
            unit = rights[iteration][HEAD:, :] / alphas[iteration]
            if iteration == 0:
                rhobar, search = alphas[0], unit
            else:
                rhobar = -cosine * alphas[iteration]
                search = unit - (sine * alphas[iteration] / rho) * search
            rho = jnp.sqrt(rhobar * rhobar + betas[iteration] * betas[iteration])
            cosine = rhobar / rho
            sine = betas[iteration] / rho
            phi = cosine * phibar
            phibar = sine * phibar
            step = (phi / rho) * search
            solution = step if iteration == 0 else solution + step
        put_slab(out, slab, solution)


def join(kernel, pieces):
    rows, width = (pieces[0].shape[0] - HEAD) // CHUNKS, 2 * FREQS * SOURCES
    joined = pl.pallas_call(
        kernel,
        out_shape=jax.ShapeDtypeStruct((rows, width), jnp.float32),
        compiler_params=pltpu.CompilerParams(vmem_limit_bytes=SMALL_VMEM_BYTES),
        cost_estimate=pl.CostEstimate(
            flops=rows * width * 4, bytes_accessed=8 * rows * width, transcendentals=0
        ),
    )(*pieces)
    return joined.reshape(rows, 2, FREQS, SOURCES)


def on_device(kernel, traces, acq_lists, counts):
    sizes = tuple(lax.axis_size(axis) for axis in ("z", "y", "x", "c"))
    row_count = kernel.shape[2] // (sizes[2] * sizes[3])
    column_count = kernel.shape[3] // (sizes[0] * sizes[1])
    aligned = row_count % 16 == 0 and column_count % 16 == 0
    moves = Neighbours() if sizes == (4, 2, 2, 2) and aligned else Whole()
    count = 2.0 * kernel.shape[2] * sizes[0] * sizes[1] * SOURCES
    observed = dispatch(traces, acq_lists, counts, row_count)
    chains = [
        chain(moves, kernel, slab, observed[slab], row_count, column_count, count)
        for slab in range(FREQS)
    ]
    rights, norms, lefts = zip(*in_slots(chains, LAG))
    row = lax.broadcasted_iota(jnp.int32, (HEAD, LANES), 0)
    sums = global_sum(jnp.where(row == 0, lefts[0][:HEAD], lefts[1][:HEAD]))
    given = [ref for pair in zip(rights, norms) for group in pair for ref in group] + [sums]
    return join(functools.partial(join_solution_kernel, count), given), join(
        join_left_kernel, lefts
    )


def solution(mesh):
    rec, src = mesh.shape["rec"], mesh.shape["src"]
    depth = src // 2
    fine = Mesh(
        mesh.devices.reshape(rec // depth, depth, depth, 2), REC + SRC
    )
    placed = (
        P(None, None, REC, SRC),
        P(SRC, REC, None, None, None),
        P(SRC, REC),
        P(SRC, REC),
    )
    return jax.shard_map(
        on_device,
        mesh=fine,
        in_specs=placed,
        out_specs=(P(SRC + REC, None, None, None), P(REC + SRC, None, None, None)),
        check_vma=False,
    )
```

```python
import functools
import jax
import jax.numpy as jnp
from jax import lax
from jax.experimental import pallas as pl
from jax.experimental.pallas import tpu as pltpu
from jax.sharding import Mesh, PartitionSpec as P

FREQS = 2
SOURCES = 256
ITERS = 2
LANES = 128
HEAD = 8
CHUNKS = 2 * SOURCES // LANES
REC = ("z", "y")
SRC = ("x", "c")
VMEM_BYTES = 42 * 2**20
SMALL_VMEM_BYTES = 12 * 2**20


def split(values):
    high = values.astype(jnp.bfloat16)
    return high, (values - high.astype(jnp.float32)).astype(jnp.bfloat16)


def dot_three(left, right, dims):
    def dot(a, b):
        return lax.dot_general(a, b, (dims, ((), ())), preferred_element_type=jnp.float32)

    return dot(left[0], right[0]) + (dot(left[0], right[1]) + dot(left[1], right[0]))


def dot_exact(chosen, values):
    total = None
    for _ in range(3):
        part = values.astype(jnp.bfloat16)
        values = values - part.astype(jnp.float32)
        term = lax.dot_general(
            chosen, part, (((0,), (0,)), ((), ())), preferred_element_type=jnp.float32
        )
        total = term if total is None else total + term
    return total


def other(axis):
    index = lax.axis_index(axis)
    return index + 1 - 2 * lax.rem(index, 2)


def product_kernel(adjoint, places, outs, k_ref, *refs):
    piece_refs = refs[: len(places)]
    out_refs = refs[len(places) : len(places) + len(outs)]
    head, sum_high, sum_low, real_high, real_low, imag_high, imag_low, total = refs[
        len(places) + len(outs) :
    ]
    step = pl.program_id(0)
    half = real_high.shape[1]

    @pl.when(step == 0)
    def _():
        sums = None
        for place, piece in zip(places, piece_refs):
            rows = (piece.shape[0] - HEAD) // CHUNKS
            at = 0 if place is None else pl.multiple_of(place() * rows, rows)
            here = pl.ds(at, rows)
            for chunk in range(CHUNKS // 2):
                lanes = slice(chunk * LANES, (chunk + 1) * LANES)
                start = HEAD + chunk * rows
                real = piece[start : start + rows, :]
                start += CHUNKS // 2 * rows
                imag = piece[start : start + rows, :]
                if adjoint:
                    imag = -imag
                sum_high[here, lanes], sum_low[here, lanes] = split(real + imag)
                real_high[here, lanes], real_low[here, lanes] = split(real)
                imag_high[here, lanes], imag_low[here, lanes] = split(imag)
            sums = piece[:HEAD, :] if sums is None else sums + piece[:HEAD, :]
        head[...] = sums

    dims = ((0,), (0,)) if adjoint else ((1,), (0,))
    k_real, k_imag = k_ref[0, 0], k_ref[1, 0]
    first = dot_three(split(k_real), (sum_high[...], sum_low[...]), dims)
    second = dot_three(split(k_imag - k_real), (real_high[...], real_low[...]), dims)
    third = dot_three(split(k_real + k_imag), (imag_high[...], imag_low[...]), dims)
    rows = first.shape[0]
    at = pl.multiple_of(step * rows, rows)
    total[pl.ds(at, rows), :half] = first - third
    total[pl.ds(at, rows), half:] = -(first + second) if adjoint else first + second

    @pl.when(step == pl.num_programs(0) - 1)
    def _():
        for out, out_ref in zip(outs, out_refs):
            for slot, place in enumerate(out):
                target = out_ref.at[slot] if len(out) > 1 else out_ref
                rows = (target.shape[0] - HEAD) // CHUNKS
                at = 0 if place is None else pl.multiple_of(place() * rows, rows)
                target[:HEAD, :] = head[...]
                for chunk in range(CHUNKS):
                    lanes = slice(chunk * LANES, (chunk + 1) * LANES)
                    start = HEAD + chunk * rows
                    target[start : start + rows, :] = total[pl.ds(at, rows), lanes]


def product(kernel, slab, adjoint, pieces, places, outs, out_rows):
    rows, columns = kernel.shape[2:]
    width = 2 * SOURCES
    if adjoint:
        tile = columns // 2 if columns % 256 == 0 and columns > 640 else columns
        steps, shape, given, made = columns // tile, (2, 1, rows, tile), rows, columns
        k_spec = pl.BlockSpec(shape, lambda i: (0, slab, 0, i))
    else:
        tile = rows // 2
        steps, shape, given, made = rows // tile, (2, 1, tile, columns), columns, rows
        k_spec = pl.BlockSpec(shape, lambda i: (0, slab, i, 0))
    shapes = [
        ((len(out),) if len(out) > 1 else ()) + (HEAD + CHUNKS * out_rows, LANES) for out in outs
    ]
    return pl.pallas_call(
        functools.partial(product_kernel, adjoint, places, outs),
        grid=(steps,),
        in_specs=[k_spec] + [pl.BlockSpec(p.shape, lambda i: (0, 0)) for p in pieces],
        out_specs=[pl.BlockSpec(s, lambda i, n=len(s): (0,) * n) for s in shapes],
        out_shape=[jax.ShapeDtypeStruct(s, jnp.float32) for s in shapes],
        scratch_shapes=[pltpu.VMEM((HEAD, LANES), jnp.float32)]
        + [pltpu.VMEM((given, SOURCES), jnp.bfloat16)] * 6
        + [pltpu.VMEM((made, width), jnp.float32)],
        compiler_params=pltpu.CompilerParams(vmem_limit_bytes=VMEM_BYTES),
        cost_estimate=pl.CostEstimate(
            flops=2 * 3 * 2 * rows * columns * width,
            bytes_accessed=8 * rows * columns + 4 * width * (rows + columns),
            transcendentals=0,
        ),
    )(kernel, *pieces)


def finish_kernel(count, parts, *refs):
    part_refs, refs = refs[:parts], refs[parts:]
    piece_ref, norm_ref = refs[-2:]
    total = part_refs[0][...]
    for part in part_refs[1:]:
        total = total + part[...]
    norm = jnp.sqrt(total[:1, :1] / count)
    data = total[HEAD:, :] / norm
    if len(refs) > 2:
        other, last_norm = refs[:2]
        data = data - norm * (other[HEAD:, :] / last_norm[:1, :1])
    piece_ref[HEAD:, :] = data
    piece_ref[:HEAD, :] = jnp.broadcast_to(jnp.sum(data * data), (HEAD, data.shape[1]))
    norm_ref[...] = jnp.broadcast_to(norm, norm_ref.shape)


def finish(count, parts, *other):
    shape = parts[0].shape
    return pl.pallas_call(
        functools.partial(finish_kernel, count, len(parts)),
        out_shape=[
            jax.ShapeDtypeStruct(shape, jnp.float32),
            jax.ShapeDtypeStruct((8, 128), jnp.float32),
        ],
        compiler_params=pltpu.CompilerParams(vmem_limit_bytes=SMALL_VMEM_BYTES),
        cost_estimate=pl.CostEstimate(
            flops=shape[0] * shape[1] * 8,
            bytes_accessed=4 * shape[0] * shape[1] * (len(parts) + 2),
            transcendentals=0,
        ),
    )(*parts, *other)


def pack_kernel(slab, place_ref, mark_ref, traces_ref, packed_ref):
    slots, width = packed_ref.shape[0], 2 * SOURCES
    spots = lax.broadcasted_iota(jnp.int32, (place_ref.shape[0], slots), 1)
    chosen = (place_ref[...] == spots).astype(jnp.bfloat16)
    for part in range(2):
        start = (part * FREQS + slab) * SOURCES
        packed_ref[:, part * SOURCES : (part + 1) * SOURCES] = dot_exact(
            chosen, traces_ref[:, start : start + SOURCES]
        )
    if packed_ref.shape[1] > width:
        marks = jnp.broadcast_to(mark_ref[...], (mark_ref.shape[0], LANES))
        packed_ref[:, width:] = dot_exact(chosen, marks)


def unpack_kernel(sources, *refs):
    mark_ref, part_refs, (piece_ref, marks, data) = refs[0], refs[1:-3], refs[-3:]
    slots, width = data.shape
    rows = (piece_ref.shape[0] - HEAD) // CHUNKS
    if sources is None:
        marks[...], data[...] = mark_ref[:, :1], part_refs[0][:, :width]
    else:
        peer = slots // len(sources)
        for index, (part, start, source) in enumerate(sources):
            here = slice(index * peer, (index + 1) * peer)
            marks[here, :] = mark_ref[pl.ds(pl.multiple_of(source() * peer, peer), peer), :1]
            data[here, :] = part_refs[part][start * peer : (start + 1) * peer, :]
    spots = lax.broadcasted_iota(jnp.int32, (slots, rows), 1) + 1
    chosen = (marks[...].astype(jnp.int32) == spots).astype(jnp.bfloat16)
    placed = dot_exact(chosen, data[...])
    for chunk in range(CHUNKS):
        start = HEAD + chunk * rows
        piece_ref[start : start + rows, :] = placed[:, chunk * LANES : (chunk + 1) * LANES]
    piece_ref[:HEAD, :] = jnp.broadcast_to(jnp.sum(placed * placed), (HEAD, LANES))


class Dispatch:
    def __init__(self, traces, acq_lists, counts, row_count):
        self.traces, self.row_count = traces.reshape(traces.shape[1], -1), row_count
        self.areas = lax.axis_size("z") * lax.axis_size("y")
        slot_count = traces.shape[1]
        self.peer = -(-slot_count // self.areas)
        ids = acq_lists[0]
        iota = jnp.arange(slot_count, dtype=jnp.int32)
        self.area = jnp.where(iota < counts[0, 0], ids // row_count, -1)
        before = (self.area[:, None] == self.area[None, :]) & (iota[None, :] < iota[:, None])
        self.rank = jnp.sum(before.astype(jnp.int32), axis=1)
        self.mark = (ids % row_count + 1).astype(jnp.float32)[:, None]

    def pack(self, slab, marked, order):
        place = jnp.where(self.area >= 0, order * self.peer + self.rank, -1)
        width = 2 * SOURCES
        slots = self.areas * self.peer
        return pl.pallas_call(
            functools.partial(pack_kernel, slab),
            out_shape=jax.ShapeDtypeStruct((slots, width + LANES * marked), jnp.float32),
            compiler_params=pltpu.CompilerParams(vmem_limit_bytes=SMALL_VMEM_BYTES),
        )(place[:, None], self.mark, self.traces)

    def exchange(self, slab, marked):
        packed = self.pack(slab, marked, self.area).reshape(self.areas, self.peer, -1)
        packed = lax.all_to_all(packed, REC, 0, 0, tiled=True)
        return packed.reshape(self.areas * self.peer, -1)

    def unpack(self, marks, parts, sources=None):
        slots, width = self.areas * self.peer, 2 * SOURCES
        shape = (HEAD + CHUNKS * self.row_count, LANES)
        return pl.pallas_call(
            functools.partial(unpack_kernel, sources),
            out_shape=jax.ShapeDtypeStruct(shape, jnp.float32),
            scratch_shapes=[
                pltpu.VMEM((slots, 1), jnp.float32),
                pltpu.VMEM((slots, width), jnp.float32),
            ],
            compiler_params=pltpu.CompilerParams(vmem_limit_bytes=SMALL_VMEM_BYTES),
        )(marks, *parts)

    def first(self):
        received = self.exchange(0, True)
        self.marks = received[:, 2 * SOURCES :]
        self.piece = self.unpack(self.marks, [received])
        return self.piece


def swap(values, axis, k=1):
    size = lax.axis_size(axis)
    return lax.ppermute(values, axis, [(i, i ^ k) for i in range(size)])


def at_end():
    index = lax.axis_index("z")
    return (index == 0) | (index == 3)


LATER = "~"
ASKED = {
    "y": lambda values: swap(values, "y"),
    "x": lambda values: swap(values, "x"),
    "c": lambda values: swap(values, "c"),
    "z": lambda values: swap(values, "z"),
    "mid": lambda values: lax.ppermute(values, "z", [(1, 2), (2, 1)]),
    "up": lambda values: swap(values, "z"),
    "down": lambda values: swap(values, "z"),
    "hold": lambda values: values,
}


def answer(asked):
    results = [None] * len(asked)
    asked = [(kind.rstrip(LATER), values) for kind, values in asked]
    kinds = [kind for kind, _ in asked]
    if "up" in kinds and "down" in kinds:
        up, down = kinds.index("up"), kinds.index("down")
        both = jnp.where(at_end(), asked[up][1], asked[down][1])
        results[up] = results[down] = swap(both, "z")
    for kind in ASKED:
        for index, (wanted, values) in enumerate(asked):
            if wanted == kind and results[index] is None:
                results[index] = ASKED[kind](values)
    return results


def line_place(kind):
    index = lax.axis_index("z")
    if kind == "own":
        return index
    if kind == "partner":
        return other("z")
    near = jnp.where(index < 2, 1, 0)
    return 1 + near if kind == "third" else 3 * near


def rec_place(kind, across):
    return lambda: line_place(kind) * 2 + (other("y") if across else lax.axis_index("y"))


def src_place(across_x, across_c):
    return lambda: (other("x") if across_x else lax.axis_index("x")) * 2 + (
        other("c") if across_c else lax.axis_index("c")
    )


def source_place(kz, ky):
    return (lax.axis_index("z") ^ kz) * 2 + (lax.axis_index("y") ^ ky)


KINDS = ("own", "partner", "third", "far")


class Neighbours:
    side = "z"
    rec_outs = [[rec_place(kind, across)] for across in (0, 1) for kind in KINDS]
    src_outs = [[src_place(0, 1), src_place(1, 1)], [src_place(1, 0)], [src_place(0, 0)]]

    def gather_src(self, own):
        x, c = yield ("x", own), ("c", own)
        return [own, x, c, swap(x, "c")], [src_place(*k) for k in ((0, 0), (1, 0), (0, 1), (1, 1))]

    def gather_rec(self, own):
        own_y, partner, mid = yield ("y~", own), ("z", own), ("mid", own)
        third, mid_two, own_y = yield ("down", mid), ("mid", partner), ("hold", own_y)
        third = jnp.where(at_end(), third, mid)
        third_y, far, own_y = yield ("y", third), ("down", mid_two), ("hold", own_y)
        far = jnp.where(at_end(), far, mid_two)
        far_y, partner_y, third_y = yield ("y", far), ("z", own_y), ("hold", third_y)
        return [own, partner, third, far, own_y, partner_y, third_y, far_y], [
            place for (place,) in self.rec_outs
        ]

    def dispatch(self, given, slab, lag):
        z, y = lax.axis_index("z"), lax.axis_index("y")
        apart = (given.area // 2) ^ z, (given.area % 2) ^ y
        packed = given.pack(slab, False, apart[1] * 4 + apart[0])
        packed, _ = lax.optimization_barrier((packed, given.piece))
        peer = given.peer
        (got,) = yield (("y", packed[4 * peer :]),)
        sent = [
            jnp.concatenate([part[k * peer : (k + 1) * peer] for part in (packed, got)])
            for k in range(4)
        ]
        near, far = yield ("z", sent[1]), ("hold", swap(sent[3], "z", 3))
        (middle,) = yield (("hold", swap(sent[2], "z", 2)),)
        for _ in range(lag - 3):
            yield ()
        parts = [far, middle, near]
        sources = [
            (part, start, lambda k=k, start=start: source_place(k, start))
            for part, k in ((0, 0), (1, 3), (2, 2), (3, 1))
            for start in range(2)
        ]
        return given.unpack(given.marks, [sent[0], *parts], sources)

    def scatter_rec(self, blocks):
        blocks = yield tuple(("hold", block) for block in blocks)
        own, partner, third, far, own_y, partner_y, third_y, far_y = blocks
        got_far, got_own_y, third_y, own_y, third = yield (
            ("y", far_y), (self.side, partner_y), ("hold", third_y), ("hold", own_y), ("hold", third),
        )
        far = far + got_far
        got_third, got_far, got_own_y, own_y, third, far = yield (
            ("y", third_y), ("up", far), ("hold", got_own_y), ("hold", own_y), ("hold", third),
            ("hold", far),
        )
        own_y = own_y + got_own_y
        third = third + got_third
        far = far + got_far
        got_own, got_third, got_partner, third = yield (
            ("y~", own_y), ("up", third), ("mid", far), ("hold", third),
        )
        partner = partner + got_partner
        third = third + got_third
        last = yield ("hold", got_own), ("z", partner), ("mid", third)
        return [own, *last]

    def scatter_src(self, blocks):
        sent, across, own = yield tuple(("hold", block) for block in blocks)
        back = swap(sent, "c")
        (far,) = yield (("x", across + back[1]),)
        return [own, back[0], far]


class Whole:
    rec_outs = [[None]]
    src_outs = [[None]]

    def gather(self, piece, axes):
        pieces = lax.all_gather(piece, axes, axis=0, tiled=False)
        data = pieces[:, HEAD:].reshape(pieces.shape[0], CHUNKS, -1, LANES)
        data = data.transpose(1, 0, 2, 3).reshape(-1, LANES)
        return [jnp.concatenate([jnp.sum(pieces[:, :HEAD], axis=0), data], axis=0)], [None]

    def scatter(self, blocks, axes):
        count = lax.axis_size(axes[0]) * lax.axis_size(axes[1])
        head = jnp.broadcast_to(blocks[0][:HEAD], (count, HEAD, LANES))
        data = blocks[0][HEAD:].reshape(CHUNKS, count, -1, LANES)
        data = data.transpose(1, 0, 2, 3).reshape(count, -1, LANES)
        both = jnp.concatenate([head, data], axis=1)
        return [lax.psum_scatter(both, axes, scatter_dimension=0, tiled=False)]

    def dispatch(self, given, slab, lag):
        (received,) = yield (("hold", given.exchange(slab, False)),)
        return given.unpack(given.marks, [received])

    def gather_src(self, piece):
        (piece,) = yield (("hold", piece),)
        return self.gather(piece, SRC)

    def gather_rec(self, piece):
        (piece,) = yield (("hold", piece),)
        return self.gather(piece, REC)

    def scatter_rec(self, blocks):
        (blocks,) = yield (("hold", blocks),)
        return self.scatter(blocks, REC)

    def scatter_src(self, blocks):
        (blocks,) = yield (("hold", blocks),)
        return self.scatter(blocks, SRC)


def global_sum(values):
    for axis in ("c", "x", "y", "z"):
        k = 1
        while k < lax.axis_size(axis):
            values = values + swap(values, axis, 2 * k - 1)
            k *= 2
    return values


LAG = 4


def in_slots(chains):
    values, results = [None] * len(chains), [None] * len(chains)
    live = list(range(len(chains)))
    while live:
        made = {}
        for index in list(live):
            try:
                made[index] = chains[index].send(values[index])
            except StopIteration as stop:
                results[index] = stop.value
                live.remove(index)
        asked = [request for requests in made.values() for request in requests]
        answers = answer(asked)
        waits = [index for index, (kind, _) in enumerate(asked) if not kind.endswith(LATER)]
        closed = lax.optimization_barrier(tuple(answers[index] for index in waits))
        for index, result in zip(waits, closed):
            answers[index] = result
        given = iter(answers)
        for index, requests in made.items():
            values[index] = tuple(next(given) for _ in requests)
    return results


def chain(moves, kernel, slab, given, row_count, column_count, count):
    def adjoint(piece):
        pieces, places = yield from moves.gather_src(piece)
        rows = column_count if len(moves.rec_outs) > 1 else kernel.shape[3]
        blocks = product(kernel, slab, True, pieces, places, moves.rec_outs, rows)
        return (yield from moves.scatter_rec(blocks))

    def forward(piece):
        pieces, places = yield from moves.gather_rec(piece)
        rows = row_count if len(moves.src_outs) > 1 else kernel.shape[2]
        blocks = product(kernel, slab, False, pieces, places, moves.src_outs, rows)
        return (yield from moves.scatter_src(blocks))

    left = given.piece if slab == 0 else (yield from moves.dispatch(given, slab, slab * LAG))
    right, beta = finish(count, (yield from adjoint(left)))
    rights, norms = [], [beta]
    for iteration in range(ITERS):
        left, alpha = finish(count, (yield from forward(right)), left, beta)
        rights.append(right)
        norms.append(alpha)
        if iteration + 1 < ITERS:
            right, beta = finish(count, (yield from adjoint(left)), right, alpha)
            norms.append(beta)
    return rights, norms, left


def put_slab(out, slab, piece):
    rows, each = out.shape[0], CHUNKS // 2
    for chunk in range(CHUNKS):
        at = (chunk // each * FREQS + slab) * SOURCES + chunk % each * LANES
        out[:, at : at + LANES] = piece[chunk * rows : (chunk + 1) * rows, :]


def join_left_kernel(*refs):
    for slab, left in enumerate(refs[:-1]):
        put_slab(refs[-1], slab, left[HEAD:, :])


def join_solution_kernel(count, *refs):
    refs, out = refs[:-1], refs[-1]
    for slab in range(FREQS):
        start = slab * 3 * ITERS
        rights = refs[start : start + ITERS]
        norms = [ref[:1, :1] for ref in refs[start + ITERS : start + 3 * ITERS]]
        norms.append(jnp.sqrt(refs[-1][slab : slab + 1, :1] / count))
        phibar, betas, alphas = norms[0], norms[2::2], norms[1::2]
        for iteration in range(ITERS):
            unit = rights[iteration][HEAD:, :] / alphas[iteration]
            if iteration == 0:
                rhobar, search = alphas[0], unit
            else:
                rhobar = -cosine * alphas[iteration]
                search = unit - (sine * alphas[iteration] / rho) * search
            rho = jnp.sqrt(rhobar * rhobar + betas[iteration] * betas[iteration])
            cosine = rhobar / rho
            sine = betas[iteration] / rho
            phi = cosine * phibar
            phibar = sine * phibar
            step = (phi / rho) * search
            solution = step if iteration == 0 else solution + step
        put_slab(out, slab, solution)


def join(kernel, pieces):
    rows, width = (pieces[0].shape[0] - HEAD) // CHUNKS, 2 * FREQS * SOURCES
    joined = pl.pallas_call(
        kernel,
        out_shape=jax.ShapeDtypeStruct((rows, width), jnp.float32),
        compiler_params=pltpu.CompilerParams(vmem_limit_bytes=SMALL_VMEM_BYTES),
        cost_estimate=pl.CostEstimate(
            flops=rows * width * 4, bytes_accessed=8 * rows * width, transcendentals=0
        ),
    )(*pieces)
    return joined.reshape(rows, 2, FREQS, SOURCES)


def on_device(kernel, traces, acq_lists, counts):
    sizes = tuple(lax.axis_size(axis) for axis in ("z", "y", "x", "c"))
    row_count = kernel.shape[2] // (sizes[2] * sizes[3])
    column_count = kernel.shape[3] // (sizes[0] * sizes[1])
    aligned = row_count % 16 == 0 and column_count % 16 == 0
    moves = Neighbours() if sizes == (4, 2, 2, 2) and aligned else Whole()
    count = 2.0 * kernel.shape[2] * sizes[0] * sizes[1] * SOURCES
    given = Dispatch(traces, acq_lists, counts, row_count)
    given.first()
    chains = [
        chain(moves, kernel, slab, given, row_count, column_count, count)
        for slab in range(FREQS)
    ]
    rights, norms, lefts = zip(*in_slots(chains))
    row = lax.broadcasted_iota(jnp.int32, (HEAD, LANES), 0)
    sums = global_sum(jnp.where(row == 0, lefts[0][:HEAD], lefts[1][:HEAD]))
    given = [ref for pair in zip(rights, norms) for group in pair for ref in group] + [sums]
    return join(functools.partial(join_solution_kernel, count), given), join(
        join_left_kernel, lefts
    )


def solution(mesh):
    rec, src = mesh.shape["rec"], mesh.shape["src"]
    depth = src // 2
    fine = Mesh(
        mesh.devices.reshape(rec // depth, depth, depth, 2), REC + SRC
    )
    placed = (
        P(None, None, REC, SRC),
        P(SRC, REC, None, None, None),
        P(SRC, REC),
        P(SRC, REC),
    )
    return jax.shard_map(
        on_device,
        mesh=fine,
        in_specs=placed,
        out_specs=(P(SRC + REC, None, None, None), P(REC + SRC, None, None, None)),
        check_vma=False,
    )
```

```python
import functools
import jax
import jax.numpy as jnp
from jax import lax
from jax.experimental import pallas as pl
from jax.experimental.pallas import tpu as pltpu
from jax.sharding import Mesh, PartitionSpec as P

FREQS = 2
SOURCES = 256
ITERS = 2
LANES = 128
HEAD = 8
CHUNKS = 2 * SOURCES // LANES
REC = ("z", "y")
SRC = ("x", "c")
VMEM_BYTES = 42 * 2**20
SMALL_VMEM_BYTES = 12 * 2**20


def split(values):
    high = values.astype(jnp.bfloat16)
    return high, (values - high.astype(jnp.float32)).astype(jnp.bfloat16)


def dot_three(left, right, dims):
    def dot(a, b):
        return lax.dot_general(a, b, (dims, ((), ())), preferred_element_type=jnp.float32)

    return dot(left[0], right[0]) + (dot(left[0], right[1]) + dot(left[1], right[0]))


def dot_exact(chosen, values, dims):
    total = None
    for _ in range(3):
        part = values.astype(jnp.bfloat16)
        values = values - part.astype(jnp.float32)
        term = lax.dot_general(
            chosen, part, (dims, ((), ())), preferred_element_type=jnp.float32
        )
        total = term if total is None else total + term
    return total


def other(axis):
    index = lax.axis_index(axis)
    return index + 1 - 2 * lax.rem(index, 2)


def product_kernel(adjoint, places, outs, k_ref, *refs):
    piece_refs = refs[: len(places)]
    out_refs = refs[len(places) : len(places) + len(outs)]
    head, sum_high, sum_low, real_high, real_low, imag_high, imag_low, total = refs[
        len(places) + len(outs) :
    ]
    step = pl.program_id(0)
    half = real_high.shape[1]

    @pl.when(step == 0)
    def _():
        sums = None
        for place, piece in zip(places, piece_refs):
            rows = (piece.shape[0] - HEAD) // CHUNKS
            at = 0 if place is None else pl.multiple_of(place() * rows, rows)
            here = pl.ds(at, rows)
            for chunk in range(CHUNKS // 2):
                lanes = slice(chunk * LANES, (chunk + 1) * LANES)
                start = HEAD + chunk * rows
                real = piece[start : start + rows, :]
                start += CHUNKS // 2 * rows
                imag = piece[start : start + rows, :]
                if adjoint:
                    imag = -imag
                sum_high[here, lanes], sum_low[here, lanes] = split(real + imag)
                real_high[here, lanes], real_low[here, lanes] = split(real)
                imag_high[here, lanes], imag_low[here, lanes] = split(imag)
            sums = piece[:HEAD, :] if sums is None else sums + piece[:HEAD, :]
        head[...] = sums

    dims = ((0,), (0,)) if adjoint else ((1,), (0,))
    k_real, k_imag = k_ref[0, 0], k_ref[1, 0]
    first = dot_three(split(k_real), (sum_high[...], sum_low[...]), dims)
    second = dot_three(split(k_imag - k_real), (real_high[...], real_low[...]), dims)
    third = dot_three(split(k_real + k_imag), (imag_high[...], imag_low[...]), dims)
    rows = first.shape[0]
    at = pl.multiple_of(step * rows, rows)
    total[pl.ds(at, rows), :half] = first - third
    total[pl.ds(at, rows), half:] = -(first + second) if adjoint else first + second

    @pl.when(step == pl.num_programs(0) - 1)
    def _():
        for out, out_ref in zip(outs, out_refs):
            for slot, place in enumerate(out):
                target = out_ref.at[slot] if len(out) > 1 else out_ref
                rows = (target.shape[0] - HEAD) // CHUNKS
                at = 0 if place is None else pl.multiple_of(place() * rows, rows)
                target[:HEAD, :] = head[...]
                for chunk in range(CHUNKS):
                    lanes = slice(chunk * LANES, (chunk + 1) * LANES)
                    start = HEAD + chunk * rows
                    target[start : start + rows, :] = total[pl.ds(at, rows), lanes]


def product(kernel, slab, adjoint, pieces, places, outs, out_rows):
    rows, columns = kernel.shape[2:]
    width = 2 * SOURCES
    if adjoint:
        tile = columns // 2 if columns % 256 == 0 and columns > 640 else columns
        steps, shape, given, made = columns // tile, (2, 1, rows, tile), rows, columns
        k_spec = pl.BlockSpec(shape, lambda i: (0, slab, 0, i))
    else:
        tile = rows // 4
        steps, shape, given, made = rows // tile, (2, 1, tile, columns), columns, rows
        k_spec = pl.BlockSpec(shape, lambda i: (0, slab, i, 0))
    shapes = [
        ((len(out),) if len(out) > 1 else ()) + (HEAD + CHUNKS * out_rows, LANES) for out in outs
    ]
    return pl.pallas_call(
        functools.partial(product_kernel, adjoint, places, outs),
        grid=(steps,),
        in_specs=[k_spec] + [pl.BlockSpec(p.shape, lambda i: (0, 0)) for p in pieces],
        out_specs=[pl.BlockSpec(s, lambda i, n=len(s): (0,) * n) for s in shapes],
        out_shape=[jax.ShapeDtypeStruct(s, jnp.float32) for s in shapes],
        scratch_shapes=[pltpu.VMEM((HEAD, LANES), jnp.float32)]
        + [pltpu.VMEM((given, SOURCES), jnp.bfloat16)] * 6
        + [pltpu.VMEM((made, width), jnp.float32)],
        compiler_params=pltpu.CompilerParams(vmem_limit_bytes=VMEM_BYTES),
        cost_estimate=pl.CostEstimate(
            flops=2 * 3 * 2 * rows * columns * width,
            bytes_accessed=8 * rows * columns + 4 * width * (rows + columns),
            transcendentals=0,
        ),
    )(kernel, *pieces)


def finish_kernel(count, parts, *refs):
    part_refs, refs = refs[:parts], refs[parts:]
    piece_ref, norm_ref = refs[-2:]
    total = part_refs[0][...]
    for part in part_refs[1:]:
        total = total + part[...]
    norm = jnp.sqrt(total[:1, :1] / count)
    data = total[HEAD:, :] / norm
    if len(refs) > 2:
        other, last_norm = refs[:2]
        data = data - norm * (other[HEAD:, :] / last_norm[:1, :1])
    piece_ref[HEAD:, :] = data
    piece_ref[:HEAD, :] = jnp.broadcast_to(jnp.sum(data * data), (HEAD, data.shape[1]))
    norm_ref[...] = jnp.broadcast_to(norm, norm_ref.shape)


def finish(count, parts, *other):
    shape = parts[0].shape
    return pl.pallas_call(
        functools.partial(finish_kernel, count, len(parts)),
        out_shape=[
            jax.ShapeDtypeStruct(shape, jnp.float32),
            jax.ShapeDtypeStruct((8, 128), jnp.float32),
        ],
        compiler_params=pltpu.CompilerParams(vmem_limit_bytes=SMALL_VMEM_BYTES),
        cost_estimate=pl.CostEstimate(
            flops=shape[0] * shape[1] * 8,
            bytes_accessed=4 * shape[0] * shape[1] * (len(parts) + 2),
            transcendentals=0,
        ),
    )(*parts, *other)


def pack_kernel(slab, place_ref, mark_ref, traces_ref, packed_ref):
    marked = len(packed_ref.shape) == 3
    width = 2 * SOURCES
    if marked:
        peer = (packed_ref.shape[1] - HEAD) // CHUNKS
        slots = packed_ref.shape[0] * peer
    else:
        slots = packed_ref.shape[0]
    spots = lax.broadcasted_iota(jnp.int32, (place_ref.shape[0], slots), 1)
    chosen = (place_ref[...] == spots).astype(jnp.bfloat16)
    if marked:
        marks = jnp.broadcast_to(mark_ref[...], (HEAD, mark_ref.shape[1])).astype(jnp.bfloat16)
        marks = jnp.dot(marks, chosen, preferred_element_type=jnp.float32)
        packed_ref[:, :HEAD, :] = jnp.zeros((packed_ref.shape[0], HEAD, LANES), jnp.float32)
        for area in range(packed_ref.shape[0]):
            packed_ref[area, :HEAD, :peer] = marks[:, area * peer : (area + 1) * peer]
    for part in range(2):
        column = (part * FREQS + slab) * SOURCES
        packed = dot_exact(chosen, traces_ref[:, column : column + SOURCES], ((0,), (0,)))
        if not marked:
            packed_ref[:, part * SOURCES : (part + 1) * SOURCES] = packed
            continue
        for chunk in range(CHUNKS // 2):
            start = HEAD + (part * CHUNKS // 2 + chunk) * peer
            lanes = slice(chunk * LANES, (chunk + 1) * LANES)
            for area in range(packed_ref.shape[0]):
                packed_ref[area, start : start + peer, :] = packed[
                    area * peer : (area + 1) * peer, lanes
                ]


def unpack_kernel(sources, peer, mark_ref, *refs):
    part_refs, (piece_ref, marks, data) = refs[:-3], refs[-3:]
    slots = data.shape[0]
    rows = (piece_ref.shape[0] - HEAD) // CHUNKS
    for index in range(slots // peer):
        here = slice(index * peer, (index + 1) * peer)
        if sources is None:
            marks[:, here] = mark_ref[index, :HEAD, :peer]
            if part_refs:
                data[here, :] = part_refs[0][here, :]
                continue
            for chunk in range(CHUNKS):
                start = HEAD + chunk * peer
                lanes = slice(chunk * LANES, (chunk + 1) * LANES)
                data[here, lanes] = mark_ref[index, start : start + peer, :]
        else:
            part, start, source = sources[index]
            marks[:, here] = mark_ref[source(), :HEAD, :peer]
            data[here, :] = part_refs[part][start * peer : (start + 1) * peer, :]
    spots = lax.broadcasted_iota(jnp.int32, (rows, slots), 0) + 1
    chosen = (marks[:1, :].astype(jnp.int32) == spots).astype(jnp.bfloat16)
    placed = dot_exact(chosen, data[...], ((1,), (0,)))
    for chunk in range(CHUNKS):
        start = HEAD + chunk * rows
        piece_ref[start : start + rows, :] = placed[:, chunk * LANES : (chunk + 1) * LANES]
    piece_ref[:HEAD, :] = jnp.broadcast_to(jnp.sum(placed * placed), (HEAD, LANES))


class Dispatch:
    def __init__(self, traces, acq_lists, counts, row_count):
        self.traces, self.row_count = traces.reshape(traces.shape[1], -1), row_count
        self.areas = lax.axis_size("z") * lax.axis_size("y")
        slot_count = traces.shape[1]
        self.peer = -(-slot_count // self.areas)
        ids = acq_lists[0]
        iota = jnp.arange(slot_count, dtype=jnp.int32)
        self.area = jnp.where(iota < counts[0, 0], ids // row_count, -1)
        before = (self.area[:, None] == self.area[None, :]) & (iota[None, :] < iota[:, None])
        self.rank = jnp.sum(before.astype(jnp.int32), axis=1)
        self.mark = (ids % row_count + 1).astype(jnp.float32)[None, :]

    def pack(self, slab, marked, order):
        place = jnp.where(self.area >= 0, order * self.peer + self.rank, -1)
        shape = (self.areas * self.peer, 2 * SOURCES)
        if marked:
            shape = (self.areas, HEAD + CHUNKS * self.peer, LANES)
        return pl.pallas_call(
            functools.partial(pack_kernel, slab),
            out_shape=jax.ShapeDtypeStruct(shape, jnp.float32),
            compiler_params=pltpu.CompilerParams(vmem_limit_bytes=SMALL_VMEM_BYTES),
        )(place[:, None], self.mark, self.traces)

    def exchange(self, slab, marked):
        packed = self.pack(slab, marked, self.area)
        if marked:
            return lax.all_to_all(packed, REC, 0, 0, tiled=True)
        packed = packed.reshape(self.areas, self.peer, -1)
        return lax.all_to_all(packed, REC, 0, 0, tiled=True).reshape(self.areas * self.peer, -1)

    def unpack(self, parts, sources=None):
        slots, width = self.areas * self.peer, 2 * SOURCES
        shape = (HEAD + CHUNKS * self.row_count, LANES)
        return pl.pallas_call(
            functools.partial(unpack_kernel, sources, self.peer),
            out_shape=jax.ShapeDtypeStruct(shape, jnp.float32),
            scratch_shapes=[
                pltpu.VMEM((HEAD, slots), jnp.float32),
                pltpu.VMEM((slots, width), jnp.float32),
            ],
            compiler_params=pltpu.CompilerParams(vmem_limit_bytes=SMALL_VMEM_BYTES),
        )(self.marks, *parts)

    def first(self):
        self.marks = self.exchange(0, True)
        self.piece = self.unpack([])
        return self.piece


def swap(values, axis, k=1):
    size = lax.axis_size(axis)
    return lax.ppermute(values, axis, [(i, i ^ k) for i in range(size)])


def at_end():
    index = lax.axis_index("z")
    return (index == 0) | (index == 3)


LATER = "~"
ASKED = {
    "y": lambda values: swap(values, "y"),
    "x": lambda values: swap(values, "x"),
    "c": lambda values: swap(values, "c"),
    "z": lambda values: swap(values, "z"),
    "mid": lambda values: lax.ppermute(values, "z", [(1, 2), (2, 1)]),
    "up": lambda values: swap(values, "z"),
    "down": lambda values: swap(values, "z"),
    "hold": lambda values: values,
}


def answer(asked):
    results = [None] * len(asked)
    asked = [(kind.rstrip(LATER), values) for kind, values in asked]
    kinds = [kind for kind, _ in asked]
    if "up" in kinds and "down" in kinds:
        up, down = kinds.index("up"), kinds.index("down")
        both = jnp.where(at_end(), asked[up][1], asked[down][1])
        results[up] = results[down] = swap(both, "z")
    for kind in ASKED:
        for index, (wanted, values) in enumerate(asked):
            if wanted == kind and results[index] is None:
                results[index] = ASKED[kind](values)
    return results


def line_place(kind):
    index = lax.axis_index("z")
    if kind == "own":
        return index
    if kind == "partner":
        return other("z")
    near = jnp.where(index < 2, 1, 0)
    return 1 + near if kind == "third" else 3 * near


def rec_place(kind, across):
    return lambda: line_place(kind) * 2 + (other("y") if across else lax.axis_index("y"))


def src_place(across_x, across_c):
    return lambda: (other("x") if across_x else lax.axis_index("x")) * 2 + (
        other("c") if across_c else lax.axis_index("c")
    )


def source_place(kz, ky):
    return (lax.axis_index("z") ^ kz) * 2 + (lax.axis_index("y") ^ ky)


KINDS = ("own", "partner", "third", "far")


class Neighbours:
    rec_outs = [[rec_place(kind, across)] for across in (0, 1) for kind in KINDS]
    src_outs = [[src_place(0, 1), src_place(1, 1)], [src_place(1, 0)], [src_place(0, 0)]]

    def gather_src(self, own):
        x, c = yield ("x", own), ("c", own)
        return [own, x, c, swap(x, "c")], [src_place(*k) for k in ((0, 0), (1, 0), (0, 1), (1, 1))]

    def gather_rec(self, own):
        own_y, partner, mid = yield ("y~", own), ("z", own), ("mid", own)
        third, mid_two, own_y = yield ("down", mid), ("mid", partner), ("hold", own_y)
        third = jnp.where(at_end(), third, mid)
        third_y, far, own_y = yield ("y", third), ("down", mid_two), ("hold", own_y)
        far = jnp.where(at_end(), far, mid_two)
        far_y, partner_y, third_y = yield ("y", far), ("z", own_y), ("hold", third_y)
        return [own, partner, third, far, own_y, partner_y, third_y, far_y], [
            place for (place,) in self.rec_outs
        ]

    def dispatch(self, given, slab, lag):
        z, y = lax.axis_index("z"), lax.axis_index("y")
        apart = (given.area // 2) ^ z, (given.area % 2) ^ y
        packed = given.pack(slab, False, apart[1] * 4 + apart[0])
        packed, _ = lax.optimization_barrier((packed, given.piece))
        peer = given.peer
        (got,) = yield (("y", packed[4 * peer :]),)
        sent = [
            jnp.concatenate([part[k * peer : (k + 1) * peer] for part in (packed, got)])
            for k in range(4)
        ]
        near, far = yield ("z", sent[1]), ("hold", swap(sent[3], "z", 3))
        (middle,) = yield (("hold", swap(sent[2], "z", 2)),)
        for _ in range(lag - 3):
            yield ()
        parts = [far, middle, near]
        sources = [
            (part, start, lambda k=k, start=start: source_place(k, start))
            for part, k in ((0, 0), (1, 3), (2, 2), (3, 1))
            for start in range(2)
        ]
        return given.unpack([sent[0], *parts], sources)

    def scatter_rec(self, blocks, alone):
        blocks = yield tuple(("hold", block) for block in blocks)
        own, partner, third, far, own_y, partner_y, third_y, far_y = blocks
        if alone:
            got_far, third_y, third = yield ("y", far_y), ("hold", third_y), ("hold", third)
            got_own_y = None
        else:
            got_far, got_own_y, third_y, third = yield (
                ("y", far_y), ("z", partner_y), ("hold", third_y), ("hold", third),
            )
        far = far + got_far
        got_third, got_far, third, far = yield (
            ("y", third_y), ("up", far), ("hold", third), ("hold", far),
        )
        third = third + got_third
        far = far + got_far
        if alone:
            got_y, got_third, got_partner, third = yield (
                ("y", partner_y), ("up", third), ("mid", far), ("hold", third),
            )
            partner = partner + got_y
        else:
            own_y = own_y + got_own_y
            got_third, got_partner, third, own_y = yield (
                ("up", third), ("mid", far), ("hold", third), ("hold", own_y),
            )
        partner = partner + got_partner
        third = third + got_third
        last = yield ("y", own_y), ("z", partner), ("mid", third)
        return [own, *last]

    def scatter_src(self, blocks):
        sent, across, own = yield tuple(("hold", block) for block in blocks)
        back = swap(sent, "c")
        (far,) = yield (("x", across + back[1]),)
        return [own, back[0], far]


class Whole:
    rec_outs = [[None]]
    src_outs = [[None]]

    def gather(self, piece, axes):
        pieces = lax.all_gather(piece, axes, axis=0, tiled=False)
        data = pieces[:, HEAD:].reshape(pieces.shape[0], CHUNKS, -1, LANES)
        data = data.transpose(1, 0, 2, 3).reshape(-1, LANES)
        return [jnp.concatenate([jnp.sum(pieces[:, :HEAD], axis=0), data], axis=0)], [None]

    def scatter(self, blocks, axes):
        count = lax.axis_size(axes[0]) * lax.axis_size(axes[1])
        head = jnp.broadcast_to(blocks[0][:HEAD], (count, HEAD, LANES))
        data = blocks[0][HEAD:].reshape(CHUNKS, count, -1, LANES)
        data = data.transpose(1, 0, 2, 3).reshape(count, -1, LANES)
        both = jnp.concatenate([head, data], axis=1)
        return [lax.psum_scatter(both, axes, scatter_dimension=0, tiled=False)]

    def dispatch(self, given, slab, lag):
        (received,) = yield (("hold", given.exchange(slab, False)),)
        return given.unpack([received])

    def gather_src(self, piece):
        (piece,) = yield (("hold", piece),)
        return self.gather(piece, SRC)

    def gather_rec(self, piece):
        (piece,) = yield (("hold", piece),)
        return self.gather(piece, REC)

    def scatter_rec(self, blocks, alone):
        (blocks,) = yield (("hold", blocks),)
        return self.scatter(blocks, REC)

    def scatter_src(self, blocks):
        (blocks,) = yield (("hold", blocks),)
        return self.scatter(blocks, SRC)


def global_sum(values):
    for axis in ("c", "x", "y", "z"):
        k = 1
        while k < lax.axis_size(axis):
            values = values + swap(values, axis, 2 * k - 1)
            k *= 2
    return values


LAG = 4


def in_slots(chains):
    values, results = [None] * len(chains), [None] * len(chains)
    live = list(range(len(chains)))
    while live:
        made = {}
        for index in list(live):
            try:
                made[index] = chains[index].send(values[index])
            except StopIteration as stop:
                results[index] = stop.value
                live.remove(index)
        asked = [request for requests in made.values() for request in requests]
        answers = answer(asked)
        waits = [index for index, (kind, _) in enumerate(asked) if not kind.endswith(LATER)]
        closed = lax.optimization_barrier(tuple(answers[index] for index in waits))
        for index, result in zip(waits, closed):
            answers[index] = result
        given = iter(answers)
        for index, requests in made.items():
            values[index] = tuple(next(given) for _ in requests)
    return results


def chain(moves, kernel, slab, given, row_count, column_count, count):
    def adjoint(piece):
        pieces, places = yield from moves.gather_src(piece)
        rows = column_count if len(moves.rec_outs) > 1 else kernel.shape[3]
        blocks = product(kernel, slab, True, pieces, places, moves.rec_outs, rows)
        return (yield from moves.scatter_rec(blocks, slab == 0))

    def forward(piece):
        pieces, places = yield from moves.gather_rec(piece)
        rows = row_count if len(moves.src_outs) > 1 else kernel.shape[2]
        blocks = product(kernel, slab, False, pieces, places, moves.src_outs, rows)
        return (yield from moves.scatter_src(blocks))

    left = given.piece if slab == 0 else (yield from moves.dispatch(given, slab, slab * LAG))
    right, beta = finish(count, (yield from adjoint(left)))
    rights, norms = [], [beta]
    for iteration in range(ITERS):
        left, alpha = finish(count, (yield from forward(right)), left, beta)
        rights.append(right)
        norms.append(alpha)
        if iteration + 1 < ITERS:
            right, beta = finish(count, (yield from adjoint(left)), right, alpha)
            norms.append(beta)
    return rights, norms, left


def put_slab(out, slab, piece):
    rows, each = out.shape[0], CHUNKS // 2
    for chunk in range(CHUNKS):
        at = chunk % each * LANES
        out[:, chunk // each, slab, at : at + LANES] = piece[chunk * rows : (chunk + 1) * rows, :]


def join_left_kernel(*refs):
    for slab, left in enumerate(refs[:-1]):
        put_slab(refs[-1], slab, left[HEAD:, :])


def join_solution_kernel(count, *refs):
    refs, out = refs[:-1], refs[-1]
    for slab in range(FREQS):
        start = slab * 3 * ITERS
        rights = refs[start : start + ITERS]
        norms = [ref[:1, :1] for ref in refs[start + ITERS : start + 3 * ITERS]]
        norms.append(jnp.sqrt(refs[-1][slab : slab + 1, :1] / count))
        phibar, betas, alphas = norms[0], norms[2::2], norms[1::2]
        for iteration in range(ITERS):
            unit = rights[iteration][HEAD:, :] / alphas[iteration]
            if iteration == 0:
                rhobar, search = alphas[0], unit
            else:
                rhobar = -cosine * alphas[iteration]
                search = unit - (sine * alphas[iteration] / rho) * search
            rho = jnp.sqrt(rhobar * rhobar + betas[iteration] * betas[iteration])
            cosine = rhobar / rho
            sine = betas[iteration] / rho
            phi = cosine * phibar
            phibar = sine * phibar
            step = (phi / rho) * search
            solution = step if iteration == 0 else solution + step
        put_slab(out, slab, solution)


def join(kernel, pieces):
    rows, width = (pieces[0].shape[0] - HEAD) // CHUNKS, 2 * FREQS * SOURCES
    return pl.pallas_call(
        kernel,
        out_shape=jax.ShapeDtypeStruct((rows, 2, FREQS, SOURCES), jnp.float32),
        compiler_params=pltpu.CompilerParams(vmem_limit_bytes=SMALL_VMEM_BYTES),
        cost_estimate=pl.CostEstimate(
            flops=rows * width * 4, bytes_accessed=8 * rows * width, transcendentals=0
        ),
    )(*pieces)


def on_device(kernel, traces, acq_lists, counts):
    sizes = tuple(lax.axis_size(axis) for axis in ("z", "y", "x", "c"))
    row_count = kernel.shape[2] // (sizes[2] * sizes[3])
    column_count = kernel.shape[3] // (sizes[0] * sizes[1])
    aligned = row_count % 16 == 0 and column_count % 16 == 0
    moves = Neighbours() if sizes == (4, 2, 2, 2) and aligned else Whole()
    count = 2.0 * kernel.shape[2] * sizes[0] * sizes[1] * SOURCES
    given = Dispatch(traces, acq_lists, counts, row_count)
    given.first()
    chains = [
        chain(moves, kernel, slab, given, row_count, column_count, count)
        for slab in range(FREQS)
    ]
    rights, norms, lefts = zip(*in_slots(chains))
    row = lax.broadcasted_iota(jnp.int32, (HEAD, LANES), 0)
    sums = global_sum(jnp.where(row == 0, lefts[0][:HEAD], lefts[1][:HEAD]))
    given = [ref for pair in zip(rights, norms) for group in pair for ref in group] + [sums]
    return join(functools.partial(join_solution_kernel, count), given), join(
        join_left_kernel, lefts
    )


def solution(mesh):
    rec, src = mesh.shape["rec"], mesh.shape["src"]
    depth = src // 2
    fine = Mesh(
        mesh.devices.reshape(rec // depth, depth, depth, 2), REC + SRC
    )
    placed = (
        P(None, None, REC, SRC),
        P(SRC, REC, None, None, None),
        P(SRC, REC),
        P(SRC, REC),
    )
    return jax.shard_map(
        on_device,
        mesh=fine,
        in_specs=placed,
        out_specs=(P(SRC + REC, None, None, None), P(REC + SRC, None, None, None)),
        check_vma=False,
    )
```
